128 devices in a mesh: dp: 4 (over x), ctx: 32 (over y, z, core).
Axes of the slice: x: 4, y: 4, z: 4, core: 2. Of those that a mesh axis runs over, the one named last changes fastest.
Arguments:
- queries: bfloat16 [4, 16384, 2048], P('dp', 'ctx'), may hold values from -6 to 6
- key_rows: bfloat16 [4, 16384, 2048], P('dp', 'ctx'), may hold values from -6 to 6
- value_rows: bfloat16 [4, 16384, 2048], P('dp', 'ctx'), may hold values from -140 to 140
- log_gate: float32 [4, 16384, 2048], P('dp', 'ctx'), may hold values from -1 to 0, as said below
- out_gate: bfloat16 [4, 16384, 2048], P('dp', 'ctx'), may hold values from -6 to 6
- cotangent: bfloat16 [4, 16384, 4096], P('dp', 'ctx'), may hold values from -0.0234375 to 0.0234375
Outputs:
- gated_hidden: bfloat16 [4, 16384, 2048], P('dp', 'ctx')
- weight_grad: float32 [2048, 4096], P('ctx')
The draws below stay inside these ranges and needn't reach their ends.
Inputs may be any that keep to these rules, and one draw needn't show every extreme that they name: `log_gate`: every entry is negative.
All inputs are finite; a program needn't handle non-finite values.
Results may differ from the reference program's by a relative error of at most 0.0036.
Values sent between devices are 32-bit elements; how exact they have to be, the bound alone decides.
No kernel may reach another device: no remote copies, remote signals or barrier semaphores. Data moves between devices by JAX's collectives and lax.ppermute only.
A program may use at most 192 MiB of HBM per device.

```python
import math
import jax
import jax.numpy as jnp
from jax import lax

H = 16
DK = 128
D = 4096
BLOCK = 64
TOK_DEV = 512
HEAD_FEATURES = 2048
SEQUENCE_COUNT = 4
SEQUENCE_LENGTH = 16384


def draw_log_gate(key, part):
    key = jax.random.fold_in(key, 11)
    keys_combined = jax.random.split(key, 9)
    fast_share = 0.5
    fast_pick = jax.random.uniform(keys_combined[0], (HEAD_FEATURES,)) < fast_share
    fast_rate = jax.random.uniform(keys_combined[1], (HEAD_FEATURES,), jnp.float32, 0.02, 0.1)
    slow_rate = jax.random.uniform(keys_combined[2], (HEAD_FEATURES,), jnp.float32, 0.05, 0.4) * (math.log(10.0) / SEQUENCE_LENGTH)
    base_rate = jnp.where(fast_pick, fast_rate, slow_rate)
    roughness = jax.random.uniform(keys_combined[3], (SEQUENCE_COUNT, SEQUENCE_LENGTH, HEAD_FEATURES), jnp.float32, 0.5, 1.5)
    device_log = jax.random.uniform(keys_combined[4], (SEQUENCE_COUNT, SEQUENCE_LENGTH // TOK_DEV, 1, HEAD_FEATURES), jnp.float32, -math.log(2.0), math.log(2.0))
    device_factor = jnp.broadcast_to(jnp.exp(device_log), (SEQUENCE_COUNT, SEQUENCE_LENGTH // TOK_DEV, TOK_DEV, HEAD_FEATURES)).reshape(SEQUENCE_COUNT, SEQUENCE_LENGTH, HEAD_FEATURES)
    value_output = -base_rate[None, None, :] * roughness * device_factor
    token_index = jnp.arange(SEQUENCE_LENGTH)
    for spike_factor in range(2):
        spike_position = jax.random.randint(keys_combined[5 + spike_factor], (SEQUENCE_COUNT,), 0, SEQUENCE_LENGTH)
        spike_loss = jax.random.uniform(keys_combined[7 + spike_factor], (SEQUENCE_COUNT, HEAD_FEATURES), jnp.float32, 0.2, 0.4)
        spike_mask = (token_index[None, :] == spike_position[:, None]).astype(jnp.float32)
        value_output = value_output + spike_mask[:, :, None] * jnp.log1p(-spike_loss)[:, None, :]
    return value_output.astype(jnp.float32)


def draw_value_rows(key, part):
    key = jax.random.fold_in(key, 12)
    keys_combined = jax.random.split(key, 3)
    base_value = jnp.clip(jax.random.normal(keys_combined[0], (SEQUENCE_COUNT, SEQUENCE_LENGTH, HEAD_FEATURES), jnp.float32), -4.0, 4.0)
    column_scale = jnp.exp(jax.random.uniform(keys_combined[1], (HEAD_FEATURES,), jnp.float32, 0.0, math.log(10.0)))
    row_scale = jnp.exp(jax.random.uniform(keys_combined[2], (SEQUENCE_COUNT, SEQUENCE_LENGTH, 1), jnp.float32, 0.0, math.log(10.0)))
    return (base_value * column_scale[None, None, :] * row_scale / 3.0).astype(jnp.bfloat16)


def level_of(stream_key, extent, shards, smallest, largest):
    def one(dim, blocks):
        draws = jax.random.uniform(jax.random.fold_in(jax.random.fold_in(stream_key, 6), dim), (blocks,), jnp.float32, smallest / len(shards), largest / len(shards))
        return jnp.repeat(jnp.exp(draws), extent[dim] // blocks).reshape((-1,) + (1,) * (len(extent) - dim - 1))

    level = one(*shards[0])
    for cut in shards[1:]:
        level = level * one(*cut)
    return level


def normal_values(rng, extent, scale, most, cuts=(), held_as=jnp.bfloat16):
    loudness = level_of(rng, extent, cuts, -0.22, 0.18) if cuts else 1.0
    values = jax.random.normal(rng, extent, jnp.float32) * scale * loudness
    return jnp.minimum(jnp.maximum(values, -most), most).astype(held_as)


def setup_inputs(seed: int = 0) -> dict:
    seeds = jax.random.split(jax.random.key(seed), 7)
    queries = normal_values(seeds[0], (SEQUENCE_COUNT, SEQUENCE_LENGTH, HEAD_FEATURES), 1.0, 6.0, ((0, 4), (1, 32)))
    key_rows = normal_values(seeds[1], (SEQUENCE_COUNT, SEQUENCE_LENGTH, HEAD_FEATURES), 1.0, 6.0, ((0, 4), (1, 32)))
    value_rows = draw_value_rows(jax.random.fold_in(seeds[6], 71), 0)
    log_gate = draw_log_gate(jax.random.fold_in(seeds[6], 71), 0)
    out_gate = normal_values(seeds[4], (SEQUENCE_COUNT, SEQUENCE_LENGTH, HEAD_FEATURES), 1.0, 6.0, ((0, 4), (1, 32)))
    cotangent = normal_values(seeds[5], (SEQUENCE_COUNT, SEQUENCE_LENGTH, D), (1.0 / (SEQUENCE_COUNT * SEQUENCE_LENGTH) ** 0.5), 0.0234375, ((0, 4), (1, 32)))
    return {"queries": queries, "key_rows": key_rows, "value_rows": value_rows, "log_gate": log_gate, "out_gate": out_gate, "cotangent": cotangent}


highest = lax.Precision.HIGHEST

def block_update(carried, pieces):
    query_blk, key_blk, value_blk, gate_blk = pieces
    cumlog = jnp.cumsum(gate_blk, axis=0)
    blockend = cumlog[-1]
    query_full = query_blk.astype(jnp.float32)
    key_full = key_blk.astype(jnp.float32)
    value_full = value_blk.astype(jnp.float32)
    query_dec = query_full * jnp.exp(cumlog)
    query_round = query_dec.astype(jnp.bfloat16).astype(jnp.float32)
    key_inc = (key_full * jnp.exp(-cumlog)).astype(jnp.bfloat16).astype(jnp.float32)
    inter_out = jnp.einsum('thc,hcv->thv', query_dec, carried, precision=highest)
    scores = jnp.einsum('thc,shc->hts', query_round, key_inc, precision=highest)
    token_index = jnp.arange(query_blk.shape[0])
    lower_mask = token_index[:, None] >= token_index[None, :]
    scores = jnp.where(lower_mask[None], scores, jnp.zeros_like(scores))
    scores = scores.astype(jnp.bfloat16).astype(jnp.float32)
    intra_out = jnp.einsum('hts,shv->thv', scores, value_full, precision=highest)
    key_end = (key_full * jnp.exp(blockend[None] - cumlog)).astype(jnp.bfloat16).astype(jnp.float32)
    updated = jnp.exp(blockend)[:, :, None] * carried + jnp.einsum('shc,shv->hcv', key_end, value_full, precision=highest)
    return (updated, inter_out + intra_out)

def as_blocks(array):
    return array.reshape(SEQUENCE_LENGTH // BLOCK, BLOCK, H, DK)

def sequence_core(pieces):
    query_seq, key_seq, value_seq, gate_seq = pieces
    blocked = (as_blocks(query_seq), as_blocks(key_seq), as_blocks(value_seq), as_blocks(gate_seq))
    carried = jnp.zeros((H, DK, DK), jnp.float32)
    ending, outputs = lax.scan(block_update, carried, blocked)
    return outputs.reshape(SEQUENCE_LENGTH, H, DK)

def reference(queries, key_rows, value_rows, log_gate, out_gate, cotangent):
    core = lax.map(sequence_core, (queries, key_rows, value_rows, log_gate))
    mean_square = lax.optimization_barrier(jnp.mean(core * core, axis=-1, keepdims=True))
    normed = (core * lax.rsqrt(mean_square + 1e-05)).reshape(SEQUENCE_COUNT, SEQUENCE_LENGTH, H * DK)
    gate_value = out_gate.astype(jnp.float32)
    swish = gate_value * jax.nn.sigmoid(gate_value)
    gated_hidden = (normed * swish).astype(jnp.bfloat16)
    flat_hidden = gated_hidden.reshape(SEQUENCE_COUNT * SEQUENCE_LENGTH, H * DK)
    flat_cotangent = cotangent.reshape(SEQUENCE_COUNT * SEQUENCE_LENGTH, D)
    weight_grad = lax.dot_general(flat_hidden, flat_cotangent, (((0,), (0,)), ((), ())), preferred_element_type=jnp.float32)
    return (gated_hidden, weight_grad)
```

```python
import functools

import jax
import jax.numpy as jnp
from jax import lax
from jax.experimental import pallas as pl
from jax.experimental.pallas import tpu as pltpu
from jax.sharding import Mesh, PartitionSpec as P

H = 16
DK = 128
D = 4096
BLOCK = 64
TOK = 512
BLOCKS = TOK // BLOCK
HALF = DK // 2
MSG = HALF + 8
COLS = 512
AXES = ("x", "y", "z", "c")
SIZES = (4, 4, 4, 2)
F32 = jnp.float32
BF16 = jnp.bfloat16
VMEM_LIMIT = 48 * 1024 * 1024

KINDS = {"y": (0, 1, 2), "z": (3, 4, 5), "x": (6, 7)}
GROUP = 2
PIECE = 4


def linear(p):
    return ((p[0] * 4 + p[1]) * 4 + p[2]) * 2 + p[3]


def places():
    return [(x, y, z, c) for x in range(4) for y in range(4) for z in range(4) for c in range(2)]


def shift_pairs(axis, by):
    at = AXES.index(axis)
    pairs = []
    for p in places():
        q = list(p)
        step = by(p[3]) if callable(by) else by
        q[at] = (q[at] + step) % SIZES[at]
        pairs.append((linear(p), linear(q)))
    return pairs


def send(array, axis, by):
    return lax.ppermute(array, AXES, shift_pairs(axis, by))


def params(grid_dims=1):
    return pltpu.CompilerParams(
        dimension_semantics=("arbitrary",) * grid_dims, vmem_limit_bytes=VMEM_LIMIT
    )


def cost(flops, nbytes, transcendentals=0):
    return pl.CostEstimate(
        flops=int(flops), bytes_accessed=int(nbytes), transcendentals=int(transcendentals)
    )


def split(a):
    high = a.astype(BF16)
    return high, (a - high.astype(F32)).astype(BF16)


def dot_nt(a, b):
    return lax.dot_general(a, b, (((1,), (1,)), ((), ())), preferred_element_type=F32)


def dot_tn(a, b):
    return lax.dot_general(a, b, (((0,), (0,)), ((), ())), preferred_element_type=F32)


def dot_nt3(ah, al, b):
    n = ah.shape[0]
    high, low = split(b)
    both = dot_nt(jnp.concatenate([ah, al], axis=0), jnp.concatenate([high, low], axis=0))
    m = b.shape[0]
    return both[:n, :m] + (both[:n, m:] + both[n:, :m])


def block_cumsum(g):
    x = g.reshape(TOK // 8, 8, DK)
    row = lax.broadcasted_iota(jnp.int32, x.shape, 1)
    for shift in (1, 2, 4):
        x = x + jnp.where(row >= shift, pltpu.roll(x, shift, 1), 0.0)
    x = x.reshape(BLOCKS, BLOCK // 8, 8, DK)
    parts = []
    run = None
    for i in range(BLOCK // 8):
        part = x[:, i]
        if run is not None:
            part = part + run
        parts.append(part)
        run = part[:, 7:8, :]
    return jnp.stack(parts, axis=1).reshape(BLOCKS, BLOCK, DK), run


def state_kernel(where_ref, k_ref, v_ref, g_ref, keep_ref, send_ref):
    first = where_ref[3] == 0
    for head in range(GROUP):
        lanes = slice(head * DK, (head + 1) * DK)
        cum, end = block_cumsum(g_ref[:, lanes])
        k = k_ref[:, lanes].astype(F32).reshape(BLOCKS, BLOCK, DK)
        kend = (k * jnp.exp(end - cum)).astype(BF16)
        decay = jnp.exp(end)
        total = end[0]
        state = None
        for j in range(BLOCKS):
            term = dot_tn(v_ref[j * BLOCK : (j + 1) * BLOCK, lanes], kend[j])
            if j:
                state = state * decay[j] + term
                total = total + end[j]
            else:
                state = term
        row = jnp.broadcast_to(jnp.exp(total), (8, DK))
        low, high = state[:HALF], state[HALF:]
        keep_ref[head, :HALF] = jnp.where(first, low, high)
        send_ref[head, :HALF] = jnp.where(first, high, low)
        keep_ref[head, HALF:] = row
        send_ref[head, HALF:] = row


def local_state(where, k, v, g):
    out = jax.ShapeDtypeStruct((H, MSG, DK), F32)
    heads = pl.BlockSpec((TOK, GROUP * DK), lambda h, w: (0, h))
    return pl.pallas_call(
        state_kernel,
        grid_spec=pltpu.PrefetchScalarGridSpec(
            num_scalar_prefetch=1,
            grid=(H // GROUP,),
            in_specs=[heads] * 3,
            out_specs=[pl.BlockSpec((GROUP, MSG, DK), lambda h, w: (h, 0, 0))] * 2,
        ),
        out_shape=[out, out],
        compiler_params=params(),
        cost_estimate=cost(2 * TOK * DK * DK * H, 10e6, TOK * DK * H),
        name="local_state",
    )(where, k, v, g)


def core_kernel(q_ref, k_ref, v_ref, g_ref, *rest):
    out_ref, high_ref, low_ref = rest[-3:]
    shape = (BLOCKS, BLOCK, DK)
    two = 2 * BLOCK
    rows = lax.broadcasted_iota(jnp.int32, (two, two), 0)
    cols = lax.broadcasted_iota(jnp.int32, (two, two), 1)
    mask = (rows >= cols) & ((rows >= BLOCK) == (cols >= BLOCK))
    for head in range(GROUP):
        lanes = slice(head * DK, (head + 1) * DK)
        cum, end = block_cumsum(g_ref[:, lanes])
        q = q_ref[:, lanes].astype(F32).reshape(shape)
        k = k_ref[:, lanes].astype(F32).reshape(shape)
        qdec = q * jnp.exp(cum)
        qround = qdec.astype(BF16)
        qrest = (qdec - qround.astype(F32)).astype(BF16)
        kinc = (k * jnp.exp(-cum)).astype(BF16)
        kend = (k * jnp.exp(end - cum)).astype(BF16)
        decay = jnp.exp(end)
        before = jnp.zeros((1, DK), F32)
        state = None
        for pair in range(BLOCKS // 2):
            span = slice(pair * two, (pair + 1) * two)
            qq = qround[2 * pair : 2 * pair + 2].reshape(two, DK)
            kk = kinc[2 * pair : 2 * pair + 2].reshape(two, DK)
            weights = jnp.where(mask, dot_nt(qq, kk), 0.0).astype(BF16)
            intra = jnp.dot(weights, v_ref[span, lanes], preferred_element_type=F32)
            for half in range(2):
                j = 2 * pair + half
                at = slice(j * BLOCK, (j + 1) * BLOCK)
                mine = intra[half * BLOCK : (half + 1) * BLOCK]
                if state is not None:
                    mine = mine + dot_nt3(qround[j], qrest[j], state)
                out_ref[at, lanes] = mine
                far = qdec[j] * jnp.exp(before)
                high, low = split(far)
                high_ref[at, lanes] = high
                low_ref[at, lanes] = low
                before = before + end[j]
                if j < BLOCKS - 1:
                    term = dot_tn(v_ref[at, lanes], kend[j])
                    state = term if state is None else state * decay[j] + term


def local_core(piece, q, k, v, g, after, earlier):
    shape = (TOK, H * DK)
    out = [jax.ShapeDtypeStruct(shape, t) for t in (F32, BF16, BF16)]
    spec = pl.BlockSpec((TOK, GROUP * DK), lambda h: (0, h + piece * (PIECE // GROUP)))
    extra = [after] + list(earlier)
    return pl.pallas_call(
        core_kernel,
        grid=(PIECE // GROUP,),
        in_specs=[spec] * 4 + [pl.BlockSpec(memory_space=pl.ANY)] * len(extra),
        out_specs=[spec] * 3,
        out_shape=out,
        input_output_aliases={5 + i: i for i in range(len(earlier))},
        compiler_params=params(),
        cost_estimate=cost(2 * TOK * DK * DK * PIECE * 8, 5e6, 4 * TOK * DK * PIECE),
        name="local_core",
    )(q, k, v, g, *extra)


def chip_kernel(where_ref, keep_ref, got_ref, *outs):
    z, c = where_ref[2], where_ref[3]
    first = c == 0
    for d in range(4):
        base = lax.rem(z + d, 4) * 4
        a = keep_ref[pl.ds(base, 4)]
        b = got_ref[pl.ds(base, 4)]
        early = jnp.where(first, a, b)
        late = jnp.where(first, b, a)
        decay = late[:, HALF : HALF + 1, :]
        outs[d][:, :HALF] = early[:, :HALF] * decay + late[:, :HALF]
        outs[d][:, HALF:] = early[:, HALF:] * late[:, HALF:]


def row_kernel(where_ref, r0, r1, r2, r3, prefix_ref, total_ref, hold):
    z = where_ref[2]
    for d, ref in enumerate((r0, r1, r2, r3)):
        hold[lax.rem(z - d + 4, 4)] = ref[...]
    state = jnp.zeros((4, HALF, DK), F32)
    decay = jnp.ones((4, 8, DK), F32)
    for i in range(4):
        prefix_ref[i, :, :HALF] = state
        prefix_ref[i, :, HALF:] = decay
        item = hold[i]
        late = item[:, HALF:]
        state = state * late[:, :1, :] + item[:, :HALF]
        decay = decay * late
    total_ref[:, :HALF] = state
    total_ref[:, HALF:] = decay


def back_kernel(where_ref, prefix_ref, r0, r1, r2, r3, *rest):
    outs, hold = rest[:4], rest[4]
    y, z = where_ref[1], where_ref[2]
    for d, ref in enumerate((r0, r1, r2, r3)):
        hold[lax.rem(y - d + 4, 4)] = ref[...]
    state = jnp.zeros((4, HALF, DK), F32)
    for i in range(3):
        item = hold[i]
        new = state * item[:, HALF : HALF + 1, :] + item[:, :HALF]
        state = jnp.where(i < y, new, state)
    for d in range(4):
        prefix = prefix_ref[lax.rem(z + d, 4)]
        outs[d][...] = state * prefix[:, HALF : HALF + 1, :] + prefix[:, :HALF]


def core_start_kernel(where_ref, keep_ref, got_ref, r0, r1, r2, r3, mine_ref, other_ref):
    z, c = where_ref[2], where_ref[3]
    first = c == 0
    for d, ref in enumerate((r0, r1, r2, r3)):
        at = pl.ds(lax.rem(z - d + 4, 4) * 4, 4)
        chip = ref[...]
        early = jnp.where(first, keep_ref[at], got_ref[at])
        second = chip * early[:, HALF : HALF + 1, :] + early[:, :HALF]
        mine_ref[at] = jnp.where(first, chip, second)
        other_ref[at] = jnp.where(first, second, chip)


def small_call(kernel, where, arrays, outs, scratch=(), after=(), name=None):
    whole = [pl.BlockSpec(memory_space=pltpu.VMEM)]
    nbytes = sum(a.size * 4 for a in arrays)
    used = 1 + len(arrays)

    def body(*refs):
        kernel(*refs[:used], *refs[used + len(after) :])

    return pl.pallas_call(
        body,
        in_specs=[pl.BlockSpec(memory_space=pltpu.SMEM)]
        + whole * len(arrays)
        + [pl.BlockSpec(memory_space=pl.ANY)] * len(after),
        out_specs=whole * len(outs),
        out_shape=[jax.ShapeDtypeStruct(s, F32) for s in outs],
        scratch_shapes=[pltpu.VMEM(s, F32) for s in scratch],
        compiler_params=pltpu.CompilerParams(vmem_limit_bytes=VMEM_LIMIT),
        cost_estimate=cost(nbytes, 2 * nbytes),
        name=name,
    )(where, *arrays, *after)


def attend(where, q, k, v, g, own):
    keep, away = local_state(where, k, v, g)
    got = send(away, "c", 1)
    wide = convert(own, F32, away)
    msg = (4, MSG, DK)
    parts = small_call(
        chip_kernel, where, (keep, got), [msg] * 4, after=[wide], name="chip_total"
    )
    wide = send(wide, "c", 1)
    arrived = [parts[0]] + [send(parts[d], "z", d) for d in (1, 2, 3)]
    local = local_core(0, q, k, v, g, parts[1], ())
    prefix, total = small_call(
        row_kernel, where, arrived, [(4,) + msg, msg], [(4,) + msg], local[:1], "row_total"
    )
    rows = [total] + [send(total, "y", d) for d in (1, 2, 3)]
    local = local_core(1, q, k, v, g, total, local)
    out = (4, HALF, DK)
    back = small_call(
        back_kernel, where, [prefix] + rows, [out] * 4, [(4,) + msg], local[:1], "row_start"
    )
    arrived = [back[0]] + [send(back[d], "z", d) for d in (1, 2, 3)]
    local = local_core(2, q, k, v, g, back[1], local)
    other = convert(wide, BF16, back[1])
    mine, theirs = small_call(
        core_start_kernel,
        where,
        [keep, got] + arrived,
        [(H, HALF, DK)] * 2,
        after=[local[0], other],
        name="core_start",
    )
    local = local_core(3, q, k, v, g, theirs, local)
    return mine, send(theirs, "c", 1), local, other


def hidden_kernel(
    where_ref, out_ref, high_ref, low_ref, mine_ref, got_ref, gate_ref, hid_ref, keep_ref, send_ref
):
    first = where_ref[3] == 0
    for head in range(GROUP):
        lanes = slice(head * DK, (head + 1) * DK)
        a, b = mine_ref[head], got_ref[head]
        state = jnp.concatenate([jnp.where(first, a, b), jnp.where(first, b, a)], axis=0)
        core = out_ref[:, lanes] + dot_nt3(high_ref[:, lanes], low_ref[:, lanes], state)
        mean = jnp.mean(core * core, axis=-1, keepdims=True)
        gate = gate_ref[:, lanes].astype(F32)
        swish = gate * (1.0 / (1.0 + jnp.exp(-gate)))
        hidden = (core * lax.rsqrt(mean + 1e-05) * swish).astype(BF16)
        hid_ref[:, lanes] = hidden
        turned = hidden.astype(F32).T
        low, high = turned[:HALF], turned[HALF:]
        rows = slice(head * HALF, (head + 1) * HALF)
        keep_ref[rows, :] = jnp.where(first, low, high).astype(BF16)
        send_ref[rows, :] = jnp.where(first, high, low)


def gated(where, local, mine, got, gate):
    spec = pl.BlockSpec((TOK, GROUP * DK), lambda h, w: (0, h))
    state = pl.BlockSpec((GROUP, HALF, DK), lambda h, w: (h, 0, 0))
    turned = pl.BlockSpec((GROUP * HALF, TOK), lambda h, w: (h, 0))
    return pl.pallas_call(
        hidden_kernel,
        grid_spec=pltpu.PrefetchScalarGridSpec(
            num_scalar_prefetch=1,
            grid=(H // GROUP,),
            in_specs=[spec, spec, spec, state, state, spec],
            out_specs=[spec, turned, turned],
        ),
        out_shape=[
            jax.ShapeDtypeStruct((TOK, H * DK), BF16),
            jax.ShapeDtypeStruct((H * HALF, TOK), BF16),
            jax.ShapeDtypeStruct((H * HALF, TOK), F32),
        ],
        compiler_params=params(),
        cost_estimate=cost(6 * TOK * DK * DK * H, 17e6, 2 * TOK * DK * H),
        name="gated_hidden",
    )(where, *local, mine, got, gate)


def convert_kernel(a_ref, after_ref, o_ref):
    o_ref[...] = a_ref[...].astype(o_ref.dtype)


def convert(a, dtype, after):
    spec = pl.BlockSpec((TOK, COLS), lambda i: (0, i))
    return pl.pallas_call(
        convert_kernel,
        grid=(D // COLS,),
        in_specs=[spec, pl.BlockSpec(memory_space=pl.ANY)],
        out_specs=spec,
        out_shape=jax.ShapeDtypeStruct(a.shape, dtype),
        compiler_params=params(),
        cost_estimate=cost(a.size, 6 * a.size),
        name="convert",
    )(a, after)


CHUNK = {"x": (4, 4, 1, 16, TOK), "y": (1, 4, 4, 16, TOK), "z": (4, 1, 4, 16, TOK)}


def chunk_spec(axis, first):
    order = ("y", "z", "x")

    def chunk(i, w):
        return tuple(w[first + i] if name == axis else 0 for name in order) + (0, 0)

    def fixed(i, w):
        return tuple(w[0] if name == axis else 0 for name in order) + (0, 0)

    return pl.BlockSpec(CHUNK[axis], chunk if first else fixed)


def product(keep, got, own, other):
    rows = 16 * 16
    return jnp.dot(
        keep.reshape(rows, TOK), own, preferred_element_type=F32
    ) + jnp.dot(got.astype(BF16).reshape(rows, TOK), other, preferred_element_type=F32)


def first_kernel(j_ref, keep_ref, got_ref, own_ref, other_ref, *outs):
    total = product(keep_ref[...], got_ref[...], own_ref[...], other_ref[...])
    for i, out in enumerate(outs):

        @pl.when(pl.program_id(0) == i)
        def _():
            out[...] = total


def first_products(axis, chunks, keep, got, own, other):
    blocks = KINDS[axis]
    cotan = pl.BlockSpec((TOK, COLS), lambda i, w: (0, blocks[0] + i))
    features = chunk_spec(axis, 0)
    return pl.pallas_call(
        first_kernel,
        grid_spec=pltpu.PrefetchScalarGridSpec(
            num_scalar_prefetch=1,
            grid=(len(blocks),),
            in_specs=[features, features, cotan, cotan],
            out_specs=[pl.BlockSpec((256, COLS), lambda i, w: (0, 0))] * len(blocks),
        ),
        out_shape=[jax.ShapeDtypeStruct((256, COLS), F32)] * len(blocks),
        compiler_params=params(),
        cost_estimate=cost(4 * 256 * TOK * COLS * len(blocks), 2e6 * len(blocks)),
        name="first_" + axis,
    )(chunks, keep, got, own, other)


def rest_kernel(j_ref, keep_ref, got_ref, own_ref, other_ref, after_ref, out_ref):
    out_ref[0] = product(keep_ref[...], got_ref[...], own_ref[...], other_ref[...])


def rest_products(axis, chunks, keep, got, own, other, after):
    blocks = KINDS[axis]
    width = COLS * len(blocks)
    cotan = pl.BlockSpec((TOK, width), lambda i, w: (0, blocks[0] // len(blocks)))
    features = chunk_spec(axis, 1)
    return pl.pallas_call(
        rest_kernel,
        grid_spec=pltpu.PrefetchScalarGridSpec(
            num_scalar_prefetch=1,
            grid=(3,),
            in_specs=[features, features, cotan, cotan, pl.BlockSpec(memory_space=pl.ANY)],
            out_specs=pl.BlockSpec((1, 256, width), lambda i, w: (i, 0, 0)),
        ),
        out_shape=jax.ShapeDtypeStruct((3, 256, width), F32),
        compiler_params=params(),
        cost_estimate=cost(12 * 256 * TOK * width, 4e6 * len(blocks)),
        name="rest_" + axis,
    )(chunks, keep, got, own, other, after)


def exchange_sum(pieces, axis, me):
    total = pieces(me)
    arrived = [send(pieces((me + d) % 4), axis, d) for d in (1, 3, 2)]
    return total + (arrived[0] + arrived[1]) + arrived[2]


def assemble_kernel(where_ref, *refs):
    out_ref = refs[-1]
    x = where_ref[0]
    n = 0
    col = 0
    for kind in KINDS:
        width = COLS * len(KINDS[kind])
        for d in (0, 1, 3, 2):
            row = pl.multiple_of(lax.rem(x - d + 4, 4) * 16, 16)
            out_ref[pl.ds(row, 16), col : col + width] = refs[n][...]
            n += 1
        col += width


def shards(queries, key_rows, value_rows, log_gate, out_gate, cotangent):
    place = {name: lax.axis_index(name) for name in AXES}
    where = jnp.stack([place[name] for name in AXES]).astype(jnp.int32)
    q, k, v, g = queries[0], key_rows[0], value_rows[0], log_gate[0]
    own = cotangent[0]

    mine, got, local, other = attend(where, q, k, v, g, own)
    hidden, keep, away = gated(where, local, mine, got, out_gate[0])
    theirs = send(away, "c", 1).reshape(4, 4, 4, 16, TOK)
    keep = keep.reshape(4, 4, 4, 16, TOK)

    step = 1 - 2 * place["c"]
    forward = lambda c: 1 - 2 * c
    held, rest, chunks = {}, {}, {}
    for axis in KINDS:
        chunks[axis] = jnp.stack([(place[axis] - step * (1 + t)) % 4 for t in range(4)]).astype(jnp.int32)
        for b, term in zip(KINDS[axis], first_products(axis, chunks[axis], keep, theirs, own, other)):
            held[b] = term
    last = held[KINDS["x"][0]]
    for axis in KINDS:
        rest[axis] = rest_products(axis, chunks[axis], keep, theirs, own, other, last)
    order = sorted(held, key=lambda b: [blocks.index(b) for blocks in KINDS.values() if b in blocks])
    for t in range(3):
        for b in order:
            axis = next(a for a in KINDS if b in KINDS[a])
            i = KINDS[axis].index(b)
            held[b] = send(held[b], axis, forward) + rest[axis][t, :, i * COLS : (i + 1) * COLS]

    x, y, z = place["x"], place["y"], place["z"]
    lead = lambda b: held[b].reshape(4, 64, COLS)
    middle = lambda b: held[b].reshape(4, 4, 16, COLS)
    pick = lambda array, i, dim: lax.dynamic_index_in_dim(array, i, dim, keepdims=False)

    def second(axis):
        blocks = KINDS[axis]
        if axis == "z":
            return lambda i: jnp.concatenate(
                [pick(middle(b), i, 1).reshape(64, COLS) for b in blocks], axis=1
            )
        return lambda i: jnp.concatenate([pick(lead(b), i, 0) for b in blocks], axis=1)

    def third(array):
        return lambda i: pick(array.reshape(4, 16, array.shape[-1]), i, 0)

    following = {"x": ("y", "z"), "y": ("z", "x"), "z": ("x", "y")}
    done = {}
    for axis in ("y", "z", "x"):
        a2, a3 = following[axis]
        part = exchange_sum(second(axis), a2, place[a2])
        done[axis] = exchange_sum(third(part), a3, place[a3])
    pieces = []
    for kind in KINDS:
        pieces += [done[kind]] + [send(done[kind], "x", d) for d in (1, 3, 2)]
    weight_grad = pl.pallas_call(
        assemble_kernel,
        in_specs=[pl.BlockSpec(memory_space=pltpu.SMEM)]
        + [pl.BlockSpec(memory_space=pltpu.VMEM)] * len(pieces),
        out_specs=pl.BlockSpec(memory_space=pltpu.VMEM),
        out_shape=jax.ShapeDtypeStruct((64, D), F32),
        compiler_params=pltpu.CompilerParams(vmem_limit_bytes=VMEM_LIMIT),
        cost_estimate=cost(64 * D, 8 * 64 * D),
        name="assemble",
    )(where, *pieces)
    return hidden[None], weight_grad


def solution(mesh):
    fine = Mesh(mesh.devices.reshape(SIZES), AXES)
    rows = P("x", ("y", "z", "c"), None)
    return jax.shard_map(
        shards,
        mesh=fine,
        in_specs=(rows,) * 6,
        out_specs=(rows, P(("y", "z", "c"), None)),
        check_vma=False,
    )
```

```python
import functools

import jax
import jax.numpy as jnp
from jax import lax
from jax.experimental import pallas as pl
from jax.experimental.pallas import tpu as pltpu
from jax.sharding import Mesh, PartitionSpec as P

H = 16
DK = 128
D = 4096
BLOCK = 64
TOK = 512
BLOCKS = TOK // BLOCK
HALF = DK // 2
MSG = HALF + 8
COLS = 512
AXES = ("x", "y", "z", "c")
SIZES = (4, 4, 4, 2)
F32 = jnp.float32
BF16 = jnp.bfloat16
VMEM_LIMIT = 60 * 1024 * 1024
PIECE_LIMIT = 24 * 1024 * 1024
PRODUCT_LIMIT = 40 * 1024 * 1024
SMALL_LIMIT = 16 * 1024 * 1024

KINDS = {"y": (0, 1, 2), "z": (3, 4, 5), "x": (6, 7)}
GROUP = 2
PIECE = 4


def linear(p):
    return ((p[0] * 4 + p[1]) * 4 + p[2]) * 2 + p[3]


def places():
    return [(x, y, z, c) for x in range(4) for y in range(4) for z in range(4) for c in range(2)]


def shift_pairs(axis, by):
    at = AXES.index(axis)
    pairs = []
    for p in places():
        q = list(p)
        step = by(p[3]) if callable(by) else by
        q[at] = (q[at] + step) % SIZES[at]
        pairs.append((linear(p), linear(q)))
    return pairs


def send(array, axis, by):
    return lax.ppermute(array, AXES, shift_pairs(axis, by))


def params(limit=VMEM_LIMIT):
    return pltpu.CompilerParams(dimension_semantics=("arbitrary",), vmem_limit_bytes=limit)


def cost(flops, nbytes, transcendentals=0):
    return pl.CostEstimate(
        flops=int(flops), bytes_accessed=int(nbytes), transcendentals=int(transcendentals)
    )


def split(a):
    high = a.astype(BF16)
    return high, (a - high.astype(F32)).astype(BF16)


def dot_nt(a, b):
    return lax.dot_general(a, b, (((1,), (1,)), ((), ())), preferred_element_type=F32)


def dot_tn(a, b):
    return lax.dot_general(a, b, (((0,), (0,)), ((), ())), preferred_element_type=F32)


def dot_nt3(ah, al, b):
    n = ah.shape[0]
    high, low = split(b)
    both = dot_nt(jnp.concatenate([ah, al], axis=0), jnp.concatenate([high, low], axis=0))
    m = b.shape[0]
    return both[:n, :m] + (both[:n, m:] + both[n:, :m])


def block_cumsum(g):
    x = g.reshape(TOK // 8, 8, DK)
    row = lax.broadcasted_iota(jnp.int32, x.shape, 1)
    for shift in (1, 2, 4):
        x = x + jnp.where(row >= shift, pltpu.roll(x, shift, 1), 0.0)
    x = x.reshape(BLOCKS, BLOCK // 8, 8, DK)
    parts = []
    run = None
    for i in range(BLOCK // 8):
        part = x[:, i]
        if run is not None:
            part = part + run
        parts.append(part)
        run = part[:, 7:8, :]
    return jnp.stack(parts, axis=1).reshape(BLOCKS, BLOCK, DK), run


def state_kernel(
    where_ref, k_ref, v_ref, g_ref, cotan_ref, keep_ref, send_ref, cum_ref, wide_ref
):
    first = where_ref[3] == 0
    wide_ref[...] = cotan_ref[...].astype(F32)
    for head in range(GROUP):
        lanes = slice(head * DK, (head + 1) * DK)
        cum, end = block_cumsum(g_ref[:, lanes])
        cum_ref[:, lanes] = cum.reshape(TOK, DK)
        k = k_ref[:, lanes].astype(F32).reshape(BLOCKS, BLOCK, DK)
        kend = (k * jnp.exp(end - cum)).astype(BF16)
        decay = jnp.exp(end)
        total = end[0]
        state = None
        for j in range(BLOCKS):
            term = dot_tn(v_ref[j * BLOCK : (j + 1) * BLOCK, lanes], kend[j])
            if j:
                state = state * decay[j] + term
                total = total + end[j]
            else:
                state = term
        row = jnp.broadcast_to(jnp.exp(total), (8, DK))
        low, high = state[:HALF], state[HALF:]
        keep_ref[head, :HALF] = jnp.where(first, low, high)
        send_ref[head, :HALF] = jnp.where(first, high, low)
        keep_ref[head, HALF:] = row
        send_ref[head, HALF:] = row


def local_state(where, k, v, g, cotan):
    out = jax.ShapeDtypeStruct((H, MSG, DK), F32)
    steps = H // GROUP
    heads = pl.BlockSpec((TOK, GROUP * DK), lambda h, w: (0, h))
    wide = pl.BlockSpec((TOK, D // steps), lambda h, w: (0, h))
    return pl.pallas_call(
        state_kernel,
        grid_spec=pltpu.PrefetchScalarGridSpec(
            num_scalar_prefetch=1,
            grid=(steps,),
            in_specs=[heads] * 3 + [wide],
            out_specs=[pl.BlockSpec((GROUP, MSG, DK), lambda h, w: (h, 0, 0))] * 2
            + [heads, wide],
        ),
        out_shape=[out, out]
        + [jax.ShapeDtypeStruct((TOK, n), F32) for n in (H * DK, D)],
        compiler_params=params(),
        cost_estimate=cost(2 * TOK * DK * DK * H, 26e6, TOK * DK * H),
        name="local_state",
    )(where, k, v, g, cotan)


def core_kernel(q_ref, k_ref, v_ref, cum_ref, *rest):
    out_ref, high_ref, low_ref, token_ref = rest[-4:]
    token_ref[...] = jnp.zeros_like(token_ref)
    shape = (BLOCKS, BLOCK, DK)
    two = 2 * BLOCK
    rows = lax.broadcasted_iota(jnp.int32, (two, two), 0)
    cols = lax.broadcasted_iota(jnp.int32, (two, two), 1)
    mask = (rows >= cols) & ((rows >= BLOCK) == (cols >= BLOCK))
    for head in range(GROUP):
        lanes = slice(head * DK, (head + 1) * DK)
        cum = cum_ref[:, lanes].reshape(shape)
        end = cum[:, BLOCK - 1 : BLOCK, :]
        q = q_ref[:, lanes].astype(F32).reshape(shape)
        k = k_ref[:, lanes].astype(F32).reshape(shape)
        qdec = q * jnp.exp(cum)
        qround = qdec.astype(BF16)
        qrest = (qdec - qround.astype(F32)).astype(BF16)
        decay = jnp.exp(end)
        kfull = k * jnp.exp(-cum)
        kinc = kfull.astype(BF16)
        kend = (kfull * decay).astype(BF16)
        before = jnp.zeros((1, DK), F32)
        state = None
        for pair in range(BLOCKS // 2):
            span = slice(pair * two, (pair + 1) * two)
            qq = qround[2 * pair : 2 * pair + 2].reshape(two, DK)
            kk = kinc[2 * pair : 2 * pair + 2].reshape(two, DK)
            weights = jnp.where(mask, dot_nt(qq, kk), 0.0).astype(BF16)
            intra = jnp.dot(weights, v_ref[span, lanes], preferred_element_type=F32)
            for half in range(2):
                j = 2 * pair + half
                at = slice(j * BLOCK, (j + 1) * BLOCK)
                mine = intra[half * BLOCK : (half + 1) * BLOCK]
                if state is not None:
                    mine = mine + dot_nt3(qround[j], qrest[j], state)
                out_ref[at, lanes] = mine
                far = qdec[j] * jnp.exp(before)
                high, low = split(far)
                high_ref[at, lanes] = high
                low_ref[at, lanes] = low
                before = before + end[j]
                if j < BLOCKS - 1:
                    term = dot_tn(v_ref[at, lanes], kend[j])
                    state = term if state is None else state * decay[j] + term


def local_core(piece, q, k, v, cum, after, earlier):
    steps = PIECE // GROUP
    spec = pl.BlockSpec((TOK, GROUP * DK), lambda h: (0, h + piece * steps))
    extra = list(earlier) + [after]
    shape = (TOK, H * DK)
    return pl.pallas_call(
        core_kernel,
        grid=(steps,),
        in_specs=[spec] * 4 + [pl.BlockSpec(memory_space=pl.ANY)] * len(extra),
        out_specs=[spec] * 3 + [pl.BlockSpec((8, DK), lambda h: (0, 0))],
        out_shape=[jax.ShapeDtypeStruct(shape, t) for t in (F32, BF16, BF16)]
        + [jax.ShapeDtypeStruct((8, DK), F32)],
        input_output_aliases={4 + i: i for i in range(len(earlier))},
        compiler_params=params(PIECE_LIMIT),
        cost_estimate=cost(2 * TOK * DK * DK * PIECE * 8, 20e6, 4 * TOK * DK * PIECE),
        name="local_core",
    )(q, k, v, cum, *extra)


def chip_kernel(where_ref, keep_ref, got_ref, wide_ref, *outs):
    z, c = where_ref[2], where_ref[3]
    first = c == 0
    for d in range(4):
        base = lax.rem(z + d, 4) * 4
        a = keep_ref[pl.ds(base, 4)]
        b = got_ref[pl.ds(base, 4)]
        early = jnp.where(first, a, b)
        late = jnp.where(first, b, a)
        decay = late[:, HALF : HALF + 1, :]
        outs[d][:, :HALF] = early[:, :HALF] * decay + late[:, :HALF]
        outs[d][:, HALF:] = early[:, HALF:] * late[:, HALF:]


def row_kernel(where_ref, r0, r1, r2, r3, prefix_ref, total_ref, hold):
    z = where_ref[2]
    for d, ref in zip((0, 1, 3, 2), (r0, r1, r2, r3)):
        hold[lax.rem(z - d + 4, 4)] = ref[...]
    state = jnp.zeros((4, HALF, DK), F32)
    decay = jnp.ones((4, 8, DK), F32)
    for i in range(4):
        prefix_ref[i, :, :HALF] = state
        prefix_ref[i, :, HALF:] = decay
        item = hold[i]
        late = item[:, HALF:]
        state = state * late[:, :1, :] + item[:, :HALF]
        decay = decay * late
    total_ref[:, :HALF] = state
    total_ref[:, HALF:] = decay


def back_kernel(where_ref, prefix_ref, r0, r1, r2, r3, *rest):
    outs, hold = rest[:4], rest[4]
    y, z = where_ref[1], where_ref[2]
    for d, ref in zip((0, 1, 3, 2), (r0, r1, r2, r3)):
        hold[lax.rem(y - d + 4, 4)] = ref[...]
    state = jnp.zeros((4, HALF, DK), F32)
    for i in range(3):
        item = hold[i]
        new = state * item[:, HALF : HALF + 1, :] + item[:, :HALF]
        state = jnp.where(i < y, new, state)
    for d in range(4):
        prefix = prefix_ref[lax.rem(z + d, 4)]
        outs[d][...] = state * prefix[:, HALF : HALF + 1, :] + prefix[:, :HALF]


def core_start_kernel(where_ref, keep_ref, got_ref, r0, r1, r2, r3, mine_ref, other_ref):
    z, c = where_ref[2], where_ref[3]
    first = c == 0
    for d, ref in zip((0, 1, 3, 2), (r0, r1, r2, r3)):
        at = pl.ds(lax.rem(z - d + 4, 4) * 4, 4)
        chip = ref[...]
        early = jnp.where(first, keep_ref[at], got_ref[at])
        second = chip * early[:, HALF : HALF + 1, :] + early[:, :HALF]
        mine_ref[at] = jnp.where(first, chip, second)
        other_ref[at] = jnp.where(first, second, chip)


def small_call(kernel, where, arrays, outs, scratch=(), after=(), name=None):
    whole = [pl.BlockSpec(memory_space=pltpu.VMEM)]
    nbytes = sum(a.size * 4 for a in arrays)
    used = 1 + len(arrays)

    def body(*refs):
        kernel(*refs[:used], *refs[used + len(after) :])

    return pl.pallas_call(
        body,
        in_specs=[pl.BlockSpec(memory_space=pltpu.SMEM)]
        + whole * len(arrays)
        + [pl.BlockSpec(memory_space=pl.ANY)] * len(after),
        out_specs=whole * len(outs),
        out_shape=[jax.ShapeDtypeStruct(s, F32) for s in outs],
        scratch_shapes=[pltpu.VMEM(s, F32) for s in scratch],
        compiler_params=pltpu.CompilerParams(vmem_limit_bytes=SMALL_LIMIT),
        cost_estimate=cost(nbytes, 2 * nbytes),
        name=name,
    )(where, *arrays, *after)


def chip_total(where, keep, got, wide):
    vmem = pl.BlockSpec(memory_space=pltpu.VMEM)
    away = pl.BlockSpec(memory_space=pl.ANY)
    return pl.pallas_call(
        chip_kernel,
        in_specs=[pl.BlockSpec(memory_space=pltpu.SMEM), vmem, vmem, away],
        out_specs=[vmem] * 4 + [away],
        out_shape=[jax.ShapeDtypeStruct((4, MSG, DK), F32)] * 4
        + [jax.ShapeDtypeStruct(wide.shape, F32)],
        input_output_aliases={3: 4},
        compiler_params=pltpu.CompilerParams(vmem_limit_bytes=VMEM_LIMIT),
        cost_estimate=cost(H * MSG * DK * 4, 16 * H * MSG * DK),
        name="chip_total",
    )(where, keep, got, wide)


def attend(where, q, k, v, g, own):
    keep, away, cum, wide = local_state(where, k, v, g, own)
    got = send(away, "c", 1)
    msg = (4, MSG, DK)
    *parts, wide = chip_total(where, keep, got, wide)
    other = send(wide, "c", 1)
    arrived = around(parts, "z")
    *local, token = local_core(0, q, k, v, cum, parts[1], ())
    prefix, total = small_call(
        row_kernel, where, arrived, [(4,) + msg, msg], [(4,) + msg], [token], "row_total"
    )
    rows = around([total] * 4, "y")
    *local, token = local_core(1, q, k, v, cum, total, local)
    out = (4, HALF, DK)
    back = small_call(
        back_kernel, where, [prefix] + rows, [out] * 4, [(4,) + msg], [token], "row_start"
    )
    arrived = around(back, "z")
    *local, token = local_core(2, q, k, v, cum, back[1], local)
    mine, theirs = small_call(
        core_start_kernel,
        where,
        [keep, got] + arrived,
        [(H, HALF, DK)] * 2,
        after=[token],
        name="core_start",
    )
    *local, token = local_core(3, q, k, v, cum, theirs, local)
    return mine, send(theirs, "c", 1), local, other


def hidden_kernel(
    where_ref, out_ref, high_ref, low_ref, mine_ref, got_ref, gate_ref, hid_ref, keep_ref, send_ref
):
    first = where_ref[3] == 0
    for head in range(GROUP):
        lanes = slice(head * DK, (head + 1) * DK)
        a, b = mine_ref[head], got_ref[head]
        state = jnp.concatenate([jnp.where(first, a, b), jnp.where(first, b, a)], axis=0)
        core = out_ref[:, lanes] + dot_nt3(high_ref[:, lanes], low_ref[:, lanes], state)
        mean = jnp.mean(core * core, axis=-1, keepdims=True)
        gate = 0.5 * gate_ref[:, lanes].astype(F32)
        swish = gate + gate * jnp.tanh(gate)
        hidden = (core * lax.rsqrt(mean + 1e-05) * swish).astype(BF16)
        hid_ref[:, lanes] = hidden
        turned = hidden.astype(F32).T
        low, high = turned[:HALF], turned[HALF:]
        rows = slice(head * HALF, (head + 1) * HALF)
        keep_ref[rows, :] = jnp.where(first, low, high).astype(BF16)
        send_ref[rows, :] = jnp.where(first, high, low)


def gated(where, local, mine, got, gate):
    spec = pl.BlockSpec((TOK, GROUP * DK), lambda h, w: (0, h))
    state = pl.BlockSpec((GROUP, HALF, DK), lambda h, w: (h, 0, 0))
    turned = pl.BlockSpec((GROUP * HALF, TOK), lambda h, w: (h, 0))
    return pl.pallas_call(
        hidden_kernel,
        grid_spec=pltpu.PrefetchScalarGridSpec(
            num_scalar_prefetch=1,
            grid=(H // GROUP,),
            in_specs=[spec, spec, spec, state, state, spec],
            out_specs=[spec, turned, turned],
        ),
        out_shape=[
            jax.ShapeDtypeStruct((TOK, H * DK), BF16),
            jax.ShapeDtypeStruct((H * HALF, TOK), BF16),
            jax.ShapeDtypeStruct((H * HALF, TOK), F32),
        ],
        compiler_params=params(PIECE_LIMIT),
        cost_estimate=cost(6 * TOK * DK * DK * H, 17e6, 2 * TOK * DK * H),
        name="gated_hidden",
    )(where, *local, mine, got, gate)


CHUNK = {"x": (4, 4, 1, 16, TOK), "y": (1, 4, 4, 16, TOK), "z": (4, 1, 4, 16, TOK)}


def product_kernel(where_ref, keep_ref, got_ref, own_ref, other_ref, *refs):
    outs, left_ref, right_ref = refs[:-2], refs[-2], refs[-1]
    block = pl.program_id(0)
    core = where_ref[3]

    def chunk(ref, axis, j):
        if axis == "y":
            return ref[j]
        if axis == "z":
            return ref[:, j]
        return ref[:, :, j]

    for axis, blocks in KINDS.items():

        @pl.when(block == blocks[0])
        def _():
            me = where_ref[AXES.index(axis)]
            for t, d in enumerate((2, 1 + 2 * core, 3 - 2 * core, 0)):
                j = lax.rem(me + d, 4)
                for part, ref in enumerate((keep_ref, got_ref)):
                    both = chunk(ref, axis, j).reshape(256, TOK).astype(BF16)
                    lanes = slice(part * TOK, (part + 1) * TOK)
                    low, high = both[:128], both[128:]
                    left_ref[256 * t : 256 * t + 128, lanes] = jnp.where(core == 0, low, high)
                    left_ref[256 * t + 128 : 256 * t + 256, lanes] = jnp.where(core == 0, high, low)

    right_ref[:TOK, :] = own_ref[...]
    right_ref[TOK:, :] = other_ref[...].astype(BF16)
    total = jnp.dot(left_ref[...], right_ref[...], preferred_element_type=F32)
    opposite, after, before, mine = (total[256 * t : 256 * (t + 1)] for t in range(4))
    for n, blocks in enumerate(KINDS.values()):
        out = outs[7 * n : 7 * (n + 1)]

        @pl.when((block >= blocks[0]) & (block <= blocks[-1]))
        def _():
            out[0][...] = opposite[:128]
            out[1][...] = opposite[128:]
            out[2][...] = after[128:]
            out[3][...] = before[:128]
            out[4][...] = after[:128]
            out[5][...] = before[128:]
            out[6][...] = mine


def products(where, keep, got, own, other):
    rows = (128,) * 6 + (256,)
    out_specs, out_shape = [], []
    for blocks in KINDS.values():

        def column(i, w, low=blocks[0], high=blocks[-1]):
            return 0, jnp.clip(i, low, high) - low

        out_specs += [pl.BlockSpec((r, COLS), column) for r in rows]
        out_shape += [jax.ShapeDtypeStruct((r, COLS * len(blocks)), F32) for r in rows]
    cotan = pl.BlockSpec((TOK, COLS), lambda i, w: (0, i))
    whole = pl.BlockSpec((4, 4, 4, 16, TOK), lambda i, w: (0, 0, 0, 0, 0))
    outs = pl.pallas_call(
        product_kernel,
        grid_spec=pltpu.PrefetchScalarGridSpec(
            num_scalar_prefetch=1,
            grid=(D // COLS,),
            in_specs=[whole, whole, cotan, cotan],
            out_specs=out_specs,
            scratch_shapes=[pltpu.VMEM((1024, 2 * TOK), BF16), pltpu.VMEM((2 * TOK, COLS), BF16)],
        ),
        out_shape=out_shape,
        compiler_params=params(PRODUCT_LIMIT),
        cost_estimate=cost(4 * 1024 * TOK * D, 32e6),
        name="products",
    )(where, keep, got, own, other)
    return {axis: outs[7 * n : 7 * (n + 1)] for n, axis in enumerate(KINDS)}


def relay_kernel(a, b, *rest):
    out, token = rest[-2:]
    out[...] = a[...] + b[...]
    token[...] = jnp.zeros_like(token)


def relay(term, arrived, after):
    rows, width = term.shape
    spec = pl.BlockSpec((rows, COLS), lambda i: (0, i))
    return pl.pallas_call(
        relay_kernel,
        grid=(width // COLS,),
        in_specs=[spec] * 2 + [pl.BlockSpec(memory_space=pl.ANY)] * len(after),
        out_specs=[spec, pl.BlockSpec((8, DK), lambda i: (0, 0))],
        out_shape=[
            jax.ShapeDtypeStruct((rows, width), F32),
            jax.ShapeDtypeStruct((8, DK), F32),
        ],
        compiler_params=params(SMALL_LIMIT),
        cost_estimate=cost(rows * width, 12 * rows * width),
        name="relay",
    )(term, arrived, *after)


def second_kernel(axis, me, where_ref, mine, a, b, c, d, *rest):
    outs, token, total = rest[:4], rest[4], rest[5]
    start = pl.multiple_of(128 * where_ref[3], 128)
    total[pl.ds(start, 128), :] = mine[:128] + (a[...] + b[...])
    total[pl.ds(128 - start, 128), :] = mine[128:] + (c[...] + d[...])
    for d in range(4):
        j = lax.rem(where_ref[me] + d, 4)
        if axis == "z":
            for y in range(4):
                row = pl.multiple_of(64 * y + 16 * j, 16)
                outs[d][16 * y : 16 * (y + 1), :] = total[pl.ds(row, 16), :]
        else:
            outs[d][...] = total[pl.ds(pl.multiple_of(64 * j, 64), 64), :]
    token[...] = jnp.zeros_like(token)


def third_kernel(me, where_ref, a, b, c, d, *rest):
    outs, token, total = rest[:4], rest[4], rest[5]
    total[...] = a[...] + (b[...] + c[...]) + d[...]
    for i in range(4):
        row = pl.multiple_of(16 * lax.rem(where_ref[me] + i, 4), 16)
        outs[i][...] = total[pl.ds(row, 16), :]
    token[...] = jnp.zeros_like(token)


def last_kernel(where_ref, *refs):
    out = refs[-1]
    col = 0
    for n in range(3):
        a, b, c, d = refs[4 * n : 4 * (n + 1)]
        width = a.shape[1]
        out[:, col : col + width] = a[...] + (b[...] + c[...]) + d[...]
        col += width


def around(pieces, axis):
    return [pieces[0]] + [send(pieces[d], axis, d) for d in (1, 3, 2)]


def assemble_kernel(where_ref, *refs):
    for ref, d in zip(refs, (0, 1, 3, 2)):
        row = pl.multiple_of(lax.rem(where_ref[0] - d + 4, 4) * 16, 16)
        refs[-1][pl.ds(row, 16), :] = ref[...]


def shards(queries, key_rows, value_rows, log_gate, out_gate, cotangent):
    place = {name: lax.axis_index(name) for name in AXES}
    where = jnp.stack([place[name] for name in AXES]).astype(jnp.int32)
    q, k, v, g = queries[0], key_rows[0], value_rows[0], log_gate[0]
    own = cotangent[0]

    mine, got, local, other = attend(where, q, k, v, g, own)
    hidden, keep, away = gated(where, local, mine, got, out_gate[0])
    theirs = send(away, "c", 1).reshape(4, 4, 4, 16, TOK)
    keep = keep.reshape(4, 4, 4, 16, TOK)

    terms = products(where, keep, theirs, own, other)
    forward = lambda c: 1 - 2 * c
    back = lambda c: 2 * c - 1
    ahead = {axis: send(terms[axis][0], axis, forward) for axis in KINDS}
    behind = {axis: send(terms[axis][1], axis, back) for axis in KINDS}
    near = {
        axis: (send(terms[axis][2], axis, forward), send(terms[axis][3], axis, back))
        for axis in KINDS
    }
    order = ("x", "y", "z")
    token = ()
    low, high = {}, {}
    for axis in order:
        term, *token = relay(terms[axis][4], ahead[axis], token)
        low[axis] = send(term, axis, forward)
    for axis in order:
        term, *token = relay(terms[axis][5], behind[axis], token)
        high[axis] = send(term, axis, back)
    held, rounds = {}, {}
    for axis in KINDS:
        held[axis] = terms[axis][6], near[axis][1], low[axis], near[axis][0], high[axis]
    following = {"x": ("y", "z"), "y": ("z", "x"), "z": ("x", "y")}
    tail = [(8, DK)]

    def second(axis, after):
        a2 = following[axis][0]
        width = COLS * len(KINDS[axis])
        kernel = functools.partial(second_kernel, axis, AXES.index(a2))
        outs = [(64, width)] * 4 + tail
        *pieces, t = small_call(kernel, where, held[axis], outs, [(256, width)], after, "second")
        return around(pieces, a2), [t]

    def third(axis, arrived, after):
        a3 = following[axis][1]
        width = COLS * len(KINDS[axis])
        kernel = functools.partial(third_kernel, AXES.index(a3))
        outs = [(16, width)] * 4 + tail
        *pieces, t = small_call(kernel, where, arrived, outs, [(64, width)], after, "third")
        return around(pieces, a3), [t]

    rounds["x"], _ = second("x", ())
    rounds["x"], _ = third("x", rounds["x"], ())
    rounds["y"], token = second("y", ())
    rounds["z"], token = second("z", token)
    rounds["y"], token = third("y", rounds["y"], token)
    rounds["z"], token = third("z", rounds["z"], token)
    (mine,) = small_call(
        last_kernel, where, [r for axis in KINDS for r in rounds[axis]], [(16, D)], name="last"
    )
    pieces = around([mine] * 4, "x")
    weight_grad = pl.pallas_call(
        assemble_kernel,
        in_specs=[pl.BlockSpec(memory_space=pltpu.SMEM)]
        + [pl.BlockSpec(memory_space=pltpu.VMEM)] * len(pieces),
        out_specs=pl.BlockSpec(memory_space=pltpu.VMEM),
        out_shape=jax.ShapeDtypeStruct((64, D), F32),
        compiler_params=pltpu.CompilerParams(vmem_limit_bytes=SMALL_LIMIT),
        cost_estimate=cost(64 * D, 8 * 64 * D),
        name="assemble",
    )(where, *pieces)
    return hidden[None], weight_grad


def solution(mesh):
    fine = Mesh(mesh.devices.reshape(SIZES), AXES)
    rows = P("x", ("y", "z", "c"), None)
    return jax.shard_map(
        shards,
        mesh=fine,
        in_specs=(rows,) * 6,
        out_specs=(rows, P(("y", "z", "c"), None)),
        check_vma=False,
    )
```

```python
import functools

import jax
import jax.numpy as jnp
from jax import lax
from jax.experimental import pallas as pl
from jax.experimental.pallas import tpu as pltpu
from jax.sharding import Mesh, PartitionSpec as P

H = 16
DK = 128
D = 4096
BLOCK = 64
TOK = 512
BLOCKS = TOK // BLOCK
HALF = DK // 2
MSG = HALF + 8
COLS = 512
AXES = ("x", "y", "z", "c")
SIZES = (4, 4, 4, 2)
F32 = jnp.float32
BF16 = jnp.bfloat16
VMEM_LIMIT = 60 * 1024 * 1024
PIECE_LIMIT = 24 * 1024 * 1024
PRODUCT_LIMIT = 28 * 1024 * 1024
SMALL_LIMIT = 16 * 1024 * 1024

KINDS = {"y": (0, 1, 2), "z": (3, 4, 5), "x": (6, 7)}
GROUP = 2
PIECE = 4


def linear(p):
    return ((p[0] * 4 + p[1]) * 4 + p[2]) * 2 + p[3]


def places():
    return [(x, y, z, c) for x in range(4) for y in range(4) for z in range(4) for c in range(2)]


def shift_pairs(axis, by):
    at = AXES.index(axis)
    pairs = []
    for p in places():
        q = list(p)
        step = by(p[3]) if callable(by) else by
        q[at] = (q[at] + step) % SIZES[at]
        pairs.append((linear(p), linear(q)))
    return pairs


def swap(array, axis, distance):
    at = AXES.index(axis)
    pairs = []
    for p in places():
        q = list(p)
        q[at] ^= distance
        pairs.append((linear(p), linear(q)))
    return lax.ppermute(array, AXES, pairs)


def send(array, axis, by):
    return lax.ppermute(array, AXES, shift_pairs(axis, by))


def params(limit=VMEM_LIMIT):
    return pltpu.CompilerParams(dimension_semantics=("arbitrary",), vmem_limit_bytes=limit)


def cost(flops, nbytes, transcendentals=0):
    return pl.CostEstimate(
        flops=int(flops), bytes_accessed=int(nbytes), transcendentals=int(transcendentals)
    )


def split(a):
    high = a.astype(BF16)
    return high, (a - high.astype(F32)).astype(BF16)


def dot_nt(a, b):
    return lax.dot_general(a, b, (((1,), (1,)), ((), ())), preferred_element_type=F32)


def dot_tn(a, b):
    return lax.dot_general(a, b, (((0,), (0,)), ((), ())), preferred_element_type=F32)


def dot_nt3(ah, al, b):
    n = ah.shape[0]
    high, low = split(b)
    both = dot_nt(jnp.concatenate([ah, al], axis=0), jnp.concatenate([high, low], axis=0))
    m = b.shape[0]
    return both[:n, :m] + (both[:n, m:] + both[n:, :m])


def block_cumsum(g):
    x = g.reshape(TOK // 8, 8, DK)
    row = lax.broadcasted_iota(jnp.int32, x.shape, 1)
    for shift in (1, 2, 4):
        x = x + jnp.where(row >= shift, pltpu.roll(x, shift, 1), 0.0)
    x = x.reshape(BLOCKS, BLOCK // 8, 8, DK)
    parts = []
    run = None
    for i in range(BLOCK // 8):
        part = x[:, i]
        if run is not None:
            part = part + run
        parts.append(part)
        run = part[:, 7:8, :]
    return jnp.stack(parts, axis=1).reshape(BLOCKS, BLOCK, DK), run


def state_kernel(
    where_ref, k_ref, v_ref, g_ref, cotan_ref, keep_ref, send_ref, cum_ref, wide_ref
):
    first = where_ref[3] == 0
    wide_ref[...] = cotan_ref[...].astype(F32)
    for head in range(GROUP):
        lanes = slice(head * DK, (head + 1) * DK)
        cum, end = block_cumsum(g_ref[:, lanes])
        cum_ref[:, lanes] = cum.reshape(TOK, DK)
        k = k_ref[:, lanes].astype(F32).reshape(BLOCKS, BLOCK, DK)
        kend = (k * jnp.exp(end - cum)).astype(BF16)
        decay = jnp.exp(end)
        total = end[0]
        state = None
        for j in range(BLOCKS):
            term = dot_tn(v_ref[j * BLOCK : (j + 1) * BLOCK, lanes], kend[j])
            if j:
                state = state * decay[j] + term
                total = total + end[j]
            else:
                state = term
        row = jnp.broadcast_to(jnp.exp(total), (8, DK))
        low, high = state[:HALF], state[HALF:]
        keep_ref[head, :HALF] = jnp.where(first, low, high)
        send_ref[head, :HALF] = jnp.where(first, high, low)
        keep_ref[head, HALF:] = row
        send_ref[head, HALF:] = row


def local_state(where, k, v, g, cotan):
    out = jax.ShapeDtypeStruct((H, MSG, DK), F32)
    steps = H // GROUP
    heads = pl.BlockSpec((TOK, GROUP * DK), lambda h, w: (0, h))
    wide = pl.BlockSpec((TOK, D // steps), lambda h, w: (0, h))
    return pl.pallas_call(
        state_kernel,
        grid_spec=pltpu.PrefetchScalarGridSpec(
            num_scalar_prefetch=1,
            grid=(steps,),
            in_specs=[heads] * 3 + [wide],
            out_specs=[pl.BlockSpec((GROUP, MSG, DK), lambda h, w: (h, 0, 0))] * 2
            + [heads, wide],
        ),
        out_shape=[out, out]
        + [jax.ShapeDtypeStruct((TOK, n), F32) for n in (H * DK, D)],
        compiler_params=params(PIECE_LIMIT),
        cost_estimate=cost(2 * TOK * DK * DK * H, 26e6, TOK * DK * H),
        name="local_state",
    )(where, k, v, g, cotan)


def core_kernel(q_ref, k_ref, v_ref, cum_ref, *rest):
    out_ref, high_ref, low_ref, token_ref = rest[-4:]
    token_ref[...] = jnp.zeros_like(token_ref)
    shape = (BLOCKS, BLOCK, DK)
    two = 2 * BLOCK
    rows = lax.broadcasted_iota(jnp.int32, (two, two), 0)
    cols = lax.broadcasted_iota(jnp.int32, (two, two), 1)
    mask = (rows >= cols) & ((rows >= BLOCK) == (cols >= BLOCK))
    for head in range(GROUP):
        lanes = slice(head * DK, (head + 1) * DK)
        cum = cum_ref[:, lanes].reshape(shape)
        end = cum[:, BLOCK - 1 : BLOCK, :]
        q = q_ref[:, lanes].astype(F32).reshape(shape)
        k = k_ref[:, lanes].astype(F32).reshape(shape)
        qdec = q * jnp.exp(cum)
        qround = qdec.astype(BF16)
        qrest = (qdec - qround.astype(F32)).astype(BF16)
        decay = jnp.exp(end)
        kfull = k * jnp.exp(-cum)
        kinc = kfull.astype(BF16)
        kend = (kfull * decay).astype(BF16)
        before = jnp.zeros((1, DK), F32)
        state = None
        for pair in range(BLOCKS // 2):
            span = slice(pair * two, (pair + 1) * two)
            qq = qround[2 * pair : 2 * pair + 2].reshape(two, DK)
            kk = kinc[2 * pair : 2 * pair + 2].reshape(two, DK)
            weights = jnp.where(mask, dot_nt(qq, kk), 0.0).astype(BF16)
            intra = jnp.dot(weights, v_ref[span, lanes], preferred_element_type=F32)
            for half in range(2):
                j = 2 * pair + half
                at = slice(j * BLOCK, (j + 1) * BLOCK)
                mine = intra[half * BLOCK : (half + 1) * BLOCK]
                if state is not None:
                    mine = mine + dot_nt3(qround[j], qrest[j], state)
                out_ref[at, lanes] = mine
                far = qdec[j] * jnp.exp(before)
                high, low = split(far)
                high_ref[at, lanes] = high
                low_ref[at, lanes] = low
                before = before + end[j]
                if j < BLOCKS - 1:
                    term = dot_tn(v_ref[at, lanes], kend[j])
                    state = term if state is None else state * decay[j] + term


def local_core(piece, q, k, v, cum, after, earlier):
    steps = PIECE // GROUP
    spec = pl.BlockSpec((TOK, GROUP * DK), lambda h: (0, h + piece * steps))
    extra = list(earlier) + [after]
    shape = (TOK, H * DK)
    return pl.pallas_call(
        core_kernel,
        grid=(steps,),
        in_specs=[spec] * 4 + [pl.BlockSpec(memory_space=pl.ANY)] * len(extra),
        out_specs=[spec] * 3 + [pl.BlockSpec((8, DK), lambda h: (0, 0))],
        out_shape=[jax.ShapeDtypeStruct(shape, t) for t in (F32, BF16, BF16)]
        + [jax.ShapeDtypeStruct((8, DK), F32)],
        input_output_aliases={4 + i: i for i in range(len(earlier))},
        compiler_params=params(PIECE_LIMIT),
        cost_estimate=cost(2 * TOK * DK * DK * PIECE * 8, 20e6, 4 * TOK * DK * PIECE),
        name="local_core",
    )(q, k, v, cum, *extra)


def chip_kernel(where_ref, keep_ref, got_ref, wide_ref, *outs):
    z, c = where_ref[2], where_ref[3]
    first = c == 0
    for d in range(4):
        base = lax.rem(z + d, 4) * 4
        a = keep_ref[pl.ds(base, 4)]
        b = got_ref[pl.ds(base, 4)]
        early = jnp.where(first, a, b)
        late = jnp.where(first, b, a)
        decay = late[:, HALF : HALF + 1, :]
        outs[d][:, :HALF] = early[:, :HALF] * decay + late[:, :HALF]
        outs[d][:, HALF:] = early[:, HALF:] * late[:, HALF:]


def row_kernel(where_ref, r0, r1, r2, r3, prefix_ref, total_ref, hold):
    z = where_ref[2]
    for d, ref in zip((0, 1, 3, 2), (r0, r1, r2, r3)):
        hold[lax.rem(z - d + 4, 4)] = ref[...]
    state = jnp.zeros((4, HALF, DK), F32)
    decay = jnp.ones((4, 8, DK), F32)
    for i in range(4):
        prefix_ref[i, :, :HALF] = state
        prefix_ref[i, :, HALF:] = decay
        item = hold[i]
        late = item[:, HALF:]
        state = state * late[:, :1, :] + item[:, :HALF]
        decay = decay * late
    total_ref[:, :HALF] = state
    total_ref[:, HALF:] = decay


def back_kernel(where_ref, prefix_ref, r0, r1, r2, r3, *rest):
    outs, hold = rest[:4], rest[4]
    y, z = where_ref[1], where_ref[2]
    for d, ref in zip((0, 1, 3, 2), (r0, r1, r2, r3)):
        hold[lax.rem(y - d + 4, 4)] = ref[...]
    state = jnp.zeros((4, HALF, DK), F32)
    for i in range(3):
        item = hold[i]
        new = state * item[:, HALF : HALF + 1, :] + item[:, :HALF]
        state = jnp.where(i < y, new, state)
    for d in range(4):
        prefix = prefix_ref[lax.rem(z + d, 4)]
        outs[d][...] = state * prefix[:, HALF : HALF + 1, :] + prefix[:, :HALF]


def core_start_kernel(where_ref, keep_ref, got_ref, r0, r1, r2, r3, mine_ref, other_ref):
    z, c = where_ref[2], where_ref[3]
    first = c == 0
    for d, ref in zip((0, 1, 3, 2), (r0, r1, r2, r3)):
        at = pl.ds(lax.rem(z - d + 4, 4) * 4, 4)
        chip = ref[...]
        early = jnp.where(first, keep_ref[at], got_ref[at])
        second = chip * early[:, HALF : HALF + 1, :] + early[:, :HALF]
        mine_ref[at] = jnp.where(first, chip, second)
        other_ref[at] = jnp.where(first, second, chip)


def small_call(kernel, where, arrays, outs, scratch=(), after=(), name=None):
    whole = [pl.BlockSpec(memory_space=pltpu.VMEM)]
    nbytes = sum(a.size * 4 for a in arrays)
    used = 1 + len(arrays)

    def body(*refs):
        kernel(*refs[:used], *refs[used + len(after) :])

    return pl.pallas_call(
        body,
        in_specs=[pl.BlockSpec(memory_space=pltpu.SMEM)]
        + whole * len(arrays)
        + [pl.BlockSpec(memory_space=pl.ANY)] * len(after),
        out_specs=whole * len(outs),
        out_shape=[jax.ShapeDtypeStruct(s, F32) for s in outs],
        scratch_shapes=[pltpu.VMEM(s, F32) for s in scratch],
        compiler_params=pltpu.CompilerParams(vmem_limit_bytes=SMALL_LIMIT),
        cost_estimate=cost(nbytes, 2 * nbytes),
        name=name,
    )(where, *arrays, *after)


def chip_total(where, keep, got, wide):
    vmem = pl.BlockSpec(memory_space=pltpu.VMEM)
    away = pl.BlockSpec(memory_space=pl.ANY)
    return pl.pallas_call(
        chip_kernel,
        in_specs=[pl.BlockSpec(memory_space=pltpu.SMEM), vmem, vmem, away],
        out_specs=[vmem] * 4 + [away],
        out_shape=[jax.ShapeDtypeStruct((4, MSG, DK), F32)] * 4
        + [jax.ShapeDtypeStruct(wide.shape, F32)],
        input_output_aliases={3: 4},
        compiler_params=pltpu.CompilerParams(vmem_limit_bytes=SMALL_LIMIT),
        cost_estimate=cost(H * MSG * DK * 4, 16 * H * MSG * DK),
        name="chip_total",
    )(where, keep, got, wide)


def attend(where, q, k, v, g, own):
    keep, away, cum, wide = local_state(where, k, v, g, own)
    got = send(away, "c", 1)
    msg = (4, MSG, DK)
    *parts, wide = chip_total(where, keep, got, wide)
    other = send(wide, "c", 1)
    arrived = around(parts, "z")
    *local, token = local_core(0, q, k, v, cum, parts[1], ())
    prefix, total = small_call(
        row_kernel, where, arrived, [(4,) + msg, msg], [(4,) + msg], [token], "row_total"
    )
    rows = around([total] * 4, "y")
    *local, token = local_core(1, q, k, v, cum, total, local)
    out = (4, HALF, DK)
    back = small_call(
        back_kernel, where, [prefix] + rows, [out] * 4, [(4,) + msg], [token], "row_start"
    )
    arrived = around(back, "z")
    *local, token = local_core(2, q, k, v, cum, back[1], local)
    mine, theirs = small_call(
        core_start_kernel,
        where,
        [keep, got] + arrived,
        [(H, HALF, DK)] * 2,
        after=[token],
        name="core_start",
    )
    *local, token = local_core(3, q, k, v, cum, theirs, local)
    return mine, send(theirs, "c", 1), local, other


def hidden_kernel(
    where_ref, out_ref, high_ref, low_ref, mine_ref, got_ref, gate_ref, hid_ref, keep_ref, send_ref
):
    first = where_ref[3] == 0
    for head in range(GROUP):
        lanes = slice(head * DK, (head + 1) * DK)
        a, b = mine_ref[head], got_ref[head]
        state = jnp.concatenate([jnp.where(first, a, b), jnp.where(first, b, a)], axis=0)
        core = out_ref[:, lanes] + dot_nt3(high_ref[:, lanes], low_ref[:, lanes], state)
        mean = jnp.mean(core * core, axis=-1, keepdims=True)
        gate = 0.5 * gate_ref[:, lanes].astype(F32)
        swish = gate + gate * jnp.tanh(gate)
        hidden = (core * lax.rsqrt(mean + 1e-05) * swish).astype(BF16)
        hid_ref[:, lanes] = hidden
        turned = hidden.astype(F32).T
        low, high = turned[:HALF], turned[HALF:]
        rows = slice(head * HALF, (head + 1) * HALF)
        keep_ref[rows, :] = jnp.where(first, low, high).astype(BF16)
        send_ref[rows, :] = jnp.where(first, high, low)


def gated(where, local, mine, got, gate):
    spec = pl.BlockSpec((TOK, GROUP * DK), lambda h, w: (0, h))
    state = pl.BlockSpec((GROUP, HALF, DK), lambda h, w: (h, 0, 0))
    turned = pl.BlockSpec((GROUP * HALF, TOK), lambda h, w: (h, 0))
    return pl.pallas_call(
        hidden_kernel,
        grid_spec=pltpu.PrefetchScalarGridSpec(
            num_scalar_prefetch=1,
            grid=(H // GROUP,),
            in_specs=[spec, spec, spec, state, state, spec],
            out_specs=[spec, turned, turned],
        ),
        out_shape=[
            jax.ShapeDtypeStruct((TOK, H * DK), BF16),
            jax.ShapeDtypeStruct((H * HALF, TOK), BF16),
            jax.ShapeDtypeStruct((H * HALF, TOK), F32),
        ],
        compiler_params=params(PIECE_LIMIT),
        cost_estimate=cost(6 * TOK * DK * DK * H, 17e6, 2 * TOK * DK * H),
        name="gated_hidden",
    )(where, *local, mine, got, gate)


CHUNK = {"x": (4, 4, 1, 16, TOK), "y": (1, 4, 4, 16, TOK), "z": (4, 1, 4, 16, TOK)}


def product_kernel(axis, where_ref, keep_ref, got_ref, own_ref, other_ref, *refs):
    outs, token_ref, left_ref, right_ref = refs[-8:-3], refs[-3], refs[-2], refs[-1]
    core = where_ref[3]
    token_ref[...] = jnp.zeros_like(token_ref)

    def chunk(ref, j):
        if axis == "y":
            return ref[j]
        if axis == "z":
            return ref[:, j]
        return ref[:, :, j]

    @pl.when(pl.program_id(0) == 0)
    def _():
        me = where_ref[AXES.index(axis)]
        for t, d in enumerate((2, 1 + 2 * core, 3 - 2 * core, 0)):
            j = lax.rem(me + d, 4)
            for part, ref in enumerate((keep_ref, got_ref)):
                both = chunk(ref, j).reshape(256, TOK).astype(BF16)
                lanes = slice(part * TOK, (part + 1) * TOK)
                low, high = both[:128], both[128:]
                left_ref[256 * t : 256 * t + 128, lanes] = jnp.where(core == 0, low, high)
                left_ref[256 * t + 128 : 256 * t + 256, lanes] = jnp.where(core == 0, high, low)

    right_ref[:TOK, :] = own_ref[...]
    right_ref[TOK:, :] = other_ref[...].astype(BF16)
    total = jnp.dot(left_ref[...], right_ref[...], preferred_element_type=F32)
    opposite, after, before, mine = (total[256 * t : 256 * (t + 1)] for t in range(4))
    outs[0][...] = opposite[:128]
    outs[1][...] = opposite[128:]
    outs[2][...] = after
    outs[3][...] = before
    outs[4][...] = mine


def products(axis, where, keep, got, own, other, after):
    blocks = KINDS[axis]
    rows = (128,) * 2 + (256,) * 3
    cotan = pl.BlockSpec((TOK, COLS), lambda i, w: (0, blocks[0] + i))
    whole = pl.BlockSpec((4, 4, 4, 16, TOK), lambda i, w: (0, 0, 0, 0, 0))
    width = COLS * len(blocks)
    return pl.pallas_call(
        functools.partial(product_kernel, axis),
        grid_spec=pltpu.PrefetchScalarGridSpec(
            num_scalar_prefetch=1,
            grid=(len(blocks),),
            in_specs=[whole, whole, cotan, cotan]
            + [pl.BlockSpec(memory_space=pl.ANY)] * len(after),
            out_specs=[pl.BlockSpec((r, COLS), lambda i, w: (0, i)) for r in rows]
            + [pl.BlockSpec((8, DK), lambda i, w: (0, 0))],
            scratch_shapes=[
                pltpu.VMEM((1024, 2 * TOK), BF16),
                pltpu.VMEM((2 * TOK, COLS), BF16),
            ],
        ),
        out_shape=[jax.ShapeDtypeStruct((r, width), F32) for r in rows]
        + [jax.ShapeDtypeStruct((8, DK), F32)],
        compiler_params=params(PRODUCT_LIMIT),
        cost_estimate=cost(4 * 1024 * TOK * width, 8000 * width),
        name="products_" + axis,
    )(where, keep, got, own, other, *after)


def relay_kernel(a, b, *rest):
    out, token = rest[-2:]
    out[...] = a[...] + b[...]
    token[...] = jnp.zeros_like(token)


def relay(term, arrived, half, after):
    width = term.shape[1]
    spec = pl.BlockSpec((128, COLS), lambda i: (half, i))
    came = pl.BlockSpec((128, COLS), lambda i: (0, i))
    return pl.pallas_call(
        relay_kernel,
        grid=(width // COLS,),
        in_specs=[spec, came] + [pl.BlockSpec(memory_space=pl.ANY)] * len(after),
        out_specs=[spec, pl.BlockSpec((8, DK), lambda i: (0, 0))],
        out_shape=[
            jax.ShapeDtypeStruct(term.shape, F32),
            jax.ShapeDtypeStruct((8, DK), F32),
        ],
        input_output_aliases={0: 0},
        compiler_params=params(SMALL_LIMIT),
        cost_estimate=cost(128 * width, 12 * 128 * width),
        name="relay",
    )(term, arrived, *after)


def second_kernel(axis, me, where_ref, mine, a, b, *rest):
    outs, token, total = rest[:4], rest[4], rest[5]
    core = where_ref[3]
    start = pl.multiple_of(128 * core, 128)
    total[pl.ds(start, 128), :] = mine[:128] + (a[:128] + b[:128])
    total[pl.ds(128 - start, 128), :] = mine[128:] + (a[128:] + b[128:])
    for t in range(4):
        j = lax.rem(where_ref[me] + jnp.where(core == 0, 7 - t, 1 + t), 4)
        if axis == "z":
            for y in range(4):
                row = pl.multiple_of(64 * y + 16 * j, 16)
                outs[t][16 * y : 16 * (y + 1), :] = total[pl.ds(row, 16), :]
        else:
            outs[t][...] = total[pl.ds(pl.multiple_of(64 * j, 64), 64), :]
    token[...] = jnp.zeros_like(token)


def add_kernel(where_ref, a, b, out, token):
    out[...] = a[...] + b[...]
    token[...] = jnp.zeros_like(token)


def halves_kernel(me, place, where_ref, a, b, keep, away, token, total):
    total[...] = a[...] + b[...]
    rows = keep.shape[0]
    row = rows * place(where_ref[me])
    keep[...] = total[pl.ds(pl.multiple_of(row, rows), rows), :]
    away[...] = total[pl.ds(pl.multiple_of(rows - row, rows), rows), :]
    token[...] = jnp.zeros_like(token)


def last_kernel(where_ref, *refs):
    out = refs[-1]
    col = 0
    for a, b in zip(refs[0:6:2], refs[1:6:2]):
        width = a.shape[1]
        out[:, col : col + width] = a[...] + b[...]
        col += width


def around(pieces, axis):
    return [pieces[0]] + [send(pieces[d], axis, d) for d in (1, 3, 2)]


def assemble_kernel(where_ref, *refs):
    for ref, d in zip(refs, (0, 1, 3, 2)):
        row = pl.multiple_of(lax.rem(where_ref[0] - d + 4, 4) * 16, 16)
        refs[-1][pl.ds(row, 16), :] = ref[...]


def shards(queries, key_rows, value_rows, log_gate, out_gate, cotangent):
    place = {name: lax.axis_index(name) for name in AXES}
    where = jnp.stack([place[name] for name in AXES]).astype(jnp.int32)
    q, k, v, g = queries[0], key_rows[0], value_rows[0], log_gate[0]
    own = cotangent[0]

    mine, got, local, other = attend(where, q, k, v, g, own)
    hidden, keep, away = gated(where, local, mine, got, out_gate[0])
    theirs = send(away, "c", 1).reshape(4, 4, 4, 16, TOK)
    keep = keep.reshape(4, 4, 4, 16, TOK)

    forward = lambda c: 1 - 2 * c
    back = lambda c: 2 * c - 1
    terms, ahead, behind, low, high = {}, {}, {}, {}, {}

    def start(axis, after):
        *t, token = products(axis, where, keep, theirs, own, other, after)
        terms[axis] = t
        ahead[axis] = send(t[0], axis, forward)
        behind[axis] = send(t[1], axis, back)
        return [token]

    def relay_low(axis, after):
        term, *token = relay(terms[axis][2], ahead[axis], 0, after)
        low[axis] = send(term, axis, forward)
        return token

    def relay_high(axis, after):
        term, *token = relay(terms[axis][3], behind[axis], 1, after)
        high[axis] = send(term, axis, back)
        return token

    token = start("y", ())
    token = start("z", token)
    token = start("x", token)
    token = relay_low("y", token)
    token = relay_low("z", token)
    token = relay_high("y", token)
    token = relay_high("z", token)
    token = relay_low("x", token)
    token = relay_high("x", token)

    following = {"x": ("y", "z"), "y": ("z", "x"), "z": ("x", "y")}
    tail = [(8, DK)]
    order = ("y", "x", "z")
    parts, came, rounds = {}, {}, {}
    for axis in order:
        a2 = following[axis][0]
        width = COLS * len(KINDS[axis])
        kernel = functools.partial(second_kernel, axis, AXES.index(a2))
        outs = [(64, width)] * 4 + tail
        ins = [terms[axis][4], low[axis], high[axis]]
        *parts[axis], t = small_call(kernel, where, ins, outs, [(256, width)], token, "second")
        came[axis] = send(parts[axis][0], a2, forward)
        token = [t]
    for step in (1, 2):
        for axis in order:
            part = parts[axis][step]
            ins = [part, came[axis]]
            part, t = small_call(add_kernel, where, ins, [part.shape] + tail, (), token, "add")
            came[axis] = send(part, following[axis][0], forward)
            token = [t]
    for axis in order:
        rounds[axis] = parts[axis][3], came[axis]
    upper, odd = (lambda p: lax.div(p, 2)), (lambda p: lax.rem(p, 2))
    for rows, distance, place_of in ((32, 2, upper), (16, 1, odd)):
        for axis in order:
            a3 = following[axis][1]
            width = COLS * len(KINDS[axis])
            kernel = functools.partial(halves_kernel, AXES.index(a3), place_of)
            outs = [(rows, width)] * 2 + tail
            keep, away, t = small_call(
                kernel, where, rounds[axis], outs, [(2 * rows, width)], token, "halves"
            )
            rounds[axis] = keep, swap(away, a3, distance)
            token = [t]
    (mine,) = small_call(
        last_kernel, where, [r for axis in KINDS for r in rounds[axis]], [(16, D)], name="last"
    )
    pieces = around([mine] * 4, "x")
    weight_grad = pl.pallas_call(
        assemble_kernel,
        in_specs=[pl.BlockSpec(memory_space=pltpu.SMEM)]
        + [pl.BlockSpec(memory_space=pltpu.VMEM)] * len(pieces),
        out_specs=pl.BlockSpec(memory_space=pltpu.VMEM),
        out_shape=jax.ShapeDtypeStruct((64, D), F32),
        compiler_params=pltpu.CompilerParams(vmem_limit_bytes=SMALL_LIMIT),
        cost_estimate=cost(64 * D, 8 * 64 * D),
        name="assemble",
    )(where, *pieces)
    return hidden[None], weight_grad


def solution(mesh):
    fine = Mesh(mesh.devices.reshape(SIZES), AXES)
    rows = P("x", ("y", "z", "c"), None)
    return jax.shard_map(
        shards,
        mesh=fine,
        in_specs=(rows,) * 6,
        out_specs=(rows, P(("y", "z", "c"), None)),
        check_vma=False,
    )
```

```python
import functools

import jax
import jax.numpy as jnp
from jax import lax
from jax.experimental import pallas as pl
from jax.experimental.pallas import tpu as pltpu
from jax.sharding import Mesh, PartitionSpec as P

H = 16
DK = 128
D = 4096
BLOCK = 64
TOK = 512
BLOCKS = TOK // BLOCK
HALF = DK // 2
MSG = HALF + 8
COLS = 512
AXES = ("x", "y", "z", "c")
SIZES = (4, 4, 4, 2)
F32 = jnp.float32
BF16 = jnp.bfloat16
VMEM_LIMIT = 60 * 1024 * 1024
PIECE_LIMIT = 24 * 1024 * 1024
PRODUCT_LIMIT = 28 * 1024 * 1024
SMALL_LIMIT = 16 * 1024 * 1024

KINDS = {"y": (0, 1, 2), "z": (3, 4, 5), "x": (6, 7)}
GROUP = 2


def linear(p):
    return ((p[0] * 4 + p[1]) * 4 + p[2]) * 2 + p[3]


def places():
    return [(x, y, z, c) for x in range(4) for y in range(4) for z in range(4) for c in range(2)]


def shift_pairs(axis, by):
    at = AXES.index(axis)
    pairs = []
    for p in places():
        q = list(p)
        step = by(p[3]) if callable(by) else by
        q[at] = (q[at] + step) % SIZES[at]
        pairs.append((linear(p), linear(q)))
    return pairs


def swap(array, axis, distance):
    at = AXES.index(axis)
    pairs = []
    for p in places():
        q = list(p)
        q[at] ^= distance
        pairs.append((linear(p), linear(q)))
    return lax.ppermute(array, AXES, pairs)


def send(array, axis, by):
    return lax.ppermute(array, AXES, shift_pairs(axis, by))


def params(limit=VMEM_LIMIT):
    return pltpu.CompilerParams(dimension_semantics=("arbitrary",), vmem_limit_bytes=limit)


def cost(flops, nbytes, transcendentals=0):
    return pl.CostEstimate(
        flops=int(flops), bytes_accessed=int(nbytes), transcendentals=int(transcendentals)
    )


def split(a):
    high = a.astype(BF16)
    return high, (a - high.astype(F32)).astype(BF16)


def dot_nt(a, b):
    return lax.dot_general(a, b, (((1,), (1,)), ((), ())), preferred_element_type=F32)


def dot_tn(a, b):
    return lax.dot_general(a, b, (((0,), (0,)), ((), ())), preferred_element_type=F32)


def dot_nt3(ah, al, b):
    n = ah.shape[0]
    high, low = split(b)
    both = dot_nt(jnp.concatenate([ah, al], axis=0), jnp.concatenate([high, low], axis=0))
    m = b.shape[0]
    return both[:n, :m] + (both[:n, m:] + both[n:, :m])


def block_cumsum(g):
    x = g.reshape(TOK // 8, 8, DK)
    row = lax.broadcasted_iota(jnp.int32, x.shape, 1)
    for shift in (1, 2, 4):
        x = x + jnp.where(row >= shift, pltpu.roll(x, shift, 1), 0.0)
    x = x.reshape(BLOCKS, BLOCK // 8, 8, DK)
    parts = []
    run = None
    for i in range(BLOCK // 8):
        part = x[:, i]
        if run is not None:
            part = part + run
        parts.append(part)
        run = part[:, 7:8, :]
    return jnp.stack(parts, axis=1).reshape(BLOCKS, BLOCK, DK), run


def state_kernel(
    where_ref, k_ref, v_ref, g_ref, cotan_ref, keep_ref, send_ref, cum_ref, wide_ref
):
    first = where_ref[3] == 0
    wide_ref[...] = cotan_ref[...].astype(F32)
    for head in range(GROUP):
        lanes = slice(head * DK, (head + 1) * DK)
        cum, end = block_cumsum(g_ref[:, lanes])
        cum_ref[:, lanes] = cum.reshape(TOK, DK)
        k = k_ref[:, lanes].astype(F32).reshape(BLOCKS, BLOCK, DK)
        kend = (k * jnp.exp(end - cum)).astype(BF16)
        decay = jnp.exp(end)
        total = end[0]
        state = None
        for j in range(BLOCKS):
            term = dot_tn(v_ref[j * BLOCK : (j + 1) * BLOCK, lanes], kend[j])
            if j:
                state = state * decay[j] + term
                total = total + end[j]
            else:
                state = term
        row = jnp.broadcast_to(jnp.exp(total), (8, DK))
        low, high = state[:HALF], state[HALF:]
        keep_ref[head, :HALF] = jnp.where(first, low, high)
        send_ref[head, :HALF] = jnp.where(first, high, low)
        keep_ref[head, HALF:] = row
        send_ref[head, HALF:] = row


def local_state(where, k, v, g, cotan):
    out = jax.ShapeDtypeStruct((H, MSG, DK), F32)
    steps = H // GROUP
    heads = pl.BlockSpec((TOK, GROUP * DK), lambda h, w: (0, h))
    wide = pl.BlockSpec((TOK, D // steps), lambda h, w: (0, h))
    return pl.pallas_call(
        state_kernel,
        grid_spec=pltpu.PrefetchScalarGridSpec(
            num_scalar_prefetch=1,
            grid=(steps,),
            in_specs=[heads] * 3 + [wide],
            out_specs=[pl.BlockSpec((GROUP, MSG, DK), lambda h, w: (h, 0, 0))] * 2
            + [heads, wide],
        ),
        out_shape=[out, out]
        + [jax.ShapeDtypeStruct((TOK, n), F32) for n in (H * DK, D)],
        compiler_params=params(PIECE_LIMIT),
        cost_estimate=cost(2 * TOK * DK * DK * H, 26e6, TOK * DK * H),
        name="local_state",
    )(where, k, v, g, cotan)


def core_kernel(q_ref, k_ref, v_ref, cum_ref, *rest):
    out_ref, high_ref, low_ref, token_ref = rest[-4:]
    token_ref[...] = jnp.zeros_like(token_ref)
    shape = (BLOCKS, BLOCK, DK)
    two = 2 * BLOCK
    rows = lax.broadcasted_iota(jnp.int32, (two, two), 0)
    cols = lax.broadcasted_iota(jnp.int32, (two, two), 1)
    mask = (rows >= cols) & ((rows >= BLOCK) == (cols >= BLOCK))
    for head in range(GROUP):
        lanes = slice(head * DK, (head + 1) * DK)
        cum = cum_ref[:, lanes].reshape(shape)
        end = cum[:, BLOCK - 1 : BLOCK, :]
        q = q_ref[:, lanes].astype(F32).reshape(shape)
        k = k_ref[:, lanes].astype(F32).reshape(shape)
        qdec = q * jnp.exp(cum)
        qround = qdec.astype(BF16)
        qrest = (qdec - qround.astype(F32)).astype(BF16)
        decay = jnp.exp(end)
        kfull = k * jnp.exp(-cum)
        kinc = kfull.astype(BF16)
        kend = (kfull * decay).astype(BF16)
        before = jnp.zeros((1, DK), F32)
        state = None
        for pair in range(BLOCKS // 2):
            span = slice(pair * two, (pair + 1) * two)
            qq = qround[2 * pair : 2 * pair + 2].reshape(two, DK)
            kk = kinc[2 * pair : 2 * pair + 2].reshape(two, DK)
            weights = jnp.where(mask, dot_nt(qq, kk), 0.0).astype(BF16)
            intra = jnp.dot(weights, v_ref[span, lanes], preferred_element_type=F32)
            for half in range(2):
                j = 2 * pair + half
                at = slice(j * BLOCK, (j + 1) * BLOCK)
                mine = intra[half * BLOCK : (half + 1) * BLOCK]
                if state is not None:
                    mine = mine + dot_nt3(qround[j], qrest[j], state)
                out_ref[at, lanes] = mine
                far = qdec[j] * jnp.exp(before)
                high, low = split(far)
                high_ref[at, lanes] = high
                low_ref[at, lanes] = low
                before = before + end[j]
                if j < BLOCKS - 1:
                    term = dot_tn(v_ref[at, lanes], kend[j])
                    state = term if state is None else state * decay[j] + term


def local_core(first, steps, q, k, v, cum, after, earlier):
    spec = pl.BlockSpec((TOK, GROUP * DK), lambda h: (0, h + first))
    extra = list(earlier) + [after]
    shape = (TOK, H * DK)
    return pl.pallas_call(
        core_kernel,
        grid=(steps,),
        in_specs=[spec] * 4 + [pl.BlockSpec(memory_space=pl.ANY)] * len(extra),
        out_specs=[spec] * 3 + [pl.BlockSpec((8, DK), lambda h: (0, 0))],
        out_shape=[jax.ShapeDtypeStruct(shape, t) for t in (F32, BF16, BF16)]
        + [jax.ShapeDtypeStruct((8, DK), F32)],
        input_output_aliases={4 + i: i for i in range(len(earlier))},
        compiler_params=params(PIECE_LIMIT),
        cost_estimate=cost(64 * TOK * DK * DK, 20e6, 16 * TOK * DK),
        name="local_core",
    )(q, k, v, cum, *extra)


def chip_kernel(where_ref, keep_ref, got_ref, wide_ref, *outs):
    z, c = where_ref[2], where_ref[3]
    first = c == 0
    for d in range(4):
        base = lax.rem(z + d, 4) * 4
        a = keep_ref[pl.ds(base, 4)]
        b = got_ref[pl.ds(base, 4)]
        early = jnp.where(first, a, b)
        late = jnp.where(first, b, a)
        decay = late[:, HALF : HALF + 1, :]
        outs[d][:, :HALF] = early[:, :HALF] * decay + late[:, :HALF]
        outs[d][:, HALF:] = early[:, HALF:] * late[:, HALF:]


def row_kernel(where_ref, r0, r1, r2, r3, prefix_ref, total_ref, hold):
    z = where_ref[2]
    for d, ref in zip((0, 1, 3, 2), (r0, r1, r2, r3)):
        hold[lax.rem(z - d + 4, 4)] = ref[...]
    state = jnp.zeros((4, HALF, DK), F32)
    decay = jnp.ones((4, 8, DK), F32)
    for i in range(4):
        prefix_ref[i, :, :HALF] = state
        prefix_ref[i, :, HALF:] = decay
        item = hold[i]
        late = item[:, HALF:]
        state = state * late[:, :1, :] + item[:, :HALF]
        decay = decay * late
    total_ref[:, :HALF] = state
    total_ref[:, HALF:] = decay


def back_kernel(where_ref, prefix_ref, r0, r1, r2, r3, *rest):
    outs, hold = rest[:4], rest[4]
    y, z = where_ref[1], where_ref[2]
    for d, ref in zip((0, 1, 3, 2), (r0, r1, r2, r3)):
        hold[lax.rem(y - d + 4, 4)] = ref[...]
    state = jnp.zeros((4, HALF, DK), F32)
    for i in range(3):
        item = hold[i]
        new = state * item[:, HALF : HALF + 1, :] + item[:, :HALF]
        state = jnp.where(i < y, new, state)
    for d in range(4):
        prefix = prefix_ref[lax.rem(z + d, 4)]
        outs[d][...] = state * prefix[:, HALF : HALF + 1, :] + prefix[:, :HALF]


def core_start_kernel(where_ref, keep_ref, got_ref, r0, r1, r2, r3, mine_ref, other_ref):
    z, c = where_ref[2], where_ref[3]
    first = c == 0
    for d, ref in zip((0, 1, 3, 2), (r0, r1, r2, r3)):
        at = pl.ds(lax.rem(z - d + 4, 4) * 4, 4)
        chip = ref[...]
        early = jnp.where(first, keep_ref[at], got_ref[at])
        second = chip * early[:, HALF : HALF + 1, :] + early[:, :HALF]
        mine_ref[at] = jnp.where(first, chip, second)
        other_ref[at] = jnp.where(first, second, chip)


def small_call(kernel, where, arrays, outs, scratch=(), after=(), name=None):
    whole = [pl.BlockSpec(memory_space=pltpu.VMEM)]
    nbytes = sum(a.size * 4 for a in arrays)
    used = 1 + len(arrays)

    def body(*refs):
        kernel(*refs[:used], *refs[used + len(after) :])

    return pl.pallas_call(
        body,
        in_specs=[pl.BlockSpec(memory_space=pltpu.SMEM)]
        + whole * len(arrays)
        + [pl.BlockSpec(memory_space=pl.ANY)] * len(after),
        out_specs=whole * len(outs),
        out_shape=[jax.ShapeDtypeStruct(s, F32) for s in outs],
        scratch_shapes=[pltpu.VMEM(s, F32) for s in scratch],
        compiler_params=pltpu.CompilerParams(vmem_limit_bytes=SMALL_LIMIT),
        cost_estimate=cost(nbytes, 2 * nbytes),
        name=name,
    )(where, *arrays, *after)


def chip_total(where, keep, got, wide):
    vmem = pl.BlockSpec(memory_space=pltpu.VMEM)
    away = pl.BlockSpec(memory_space=pl.ANY)
    return pl.pallas_call(
        chip_kernel,
        in_specs=[pl.BlockSpec(memory_space=pltpu.SMEM), vmem, vmem, away],
        out_specs=[vmem] * 4 + [away],
        out_shape=[jax.ShapeDtypeStruct((4, MSG, DK), F32)] * 4
        + [jax.ShapeDtypeStruct(wide.shape, F32)],
        input_output_aliases={3: 4},
        compiler_params=pltpu.CompilerParams(vmem_limit_bytes=SMALL_LIMIT),
        cost_estimate=cost(H * MSG * DK * 4, 16 * H * MSG * DK),
        name="chip_total",
    )(where, keep, got, wide)


def attend(where, q, k, v, g, own):
    keep, away, cum, wide = local_state(where, k, v, g, own)
    got = send(away, "c", 1)
    msg = (4, MSG, DK)
    *parts, wide = chip_total(where, keep, got, wide)
    other = send(wide, "c", 1)
    arrived = around(parts, "z")
    *local, token = local_core(0, 3, q, k, v, cum, parts[1], ())
    prefix, total = small_call(
        row_kernel, where, arrived, [(4,) + msg, msg], [(4,) + msg], [token], "row_total"
    )
    rows = around([total] * 4, "y")
    *local, token = local_core(3, 2, q, k, v, cum, total, local)
    out = (4, HALF, DK)
    back = small_call(
        back_kernel, where, [prefix] + rows, [out] * 4, [(4,) + msg], [token], "row_start"
    )
    arrived = around(back, "z")
    *local, token = local_core(5, 2, q, k, v, cum, back[1], local)
    mine, theirs = small_call(
        core_start_kernel,
        where,
        [keep, got] + arrived,
        [(H, HALF, DK)] * 2,
        after=[token],
        name="core_start",
    )
    *local, token = local_core(7, 1, q, k, v, cum, theirs, local)
    return mine, send(theirs, "c", 1), local, other


def hidden_kernel(
    where_ref, out_ref, high_ref, low_ref, mine_ref, got_ref, gate_ref, hid_ref, keep_ref, send_ref
):
    first = where_ref[3] == 0
    for head in range(GROUP):
        lanes = slice(head * DK, (head + 1) * DK)
        a, b = mine_ref[head], got_ref[head]
        state = jnp.concatenate([jnp.where(first, a, b), jnp.where(first, b, a)], axis=0)
        core = out_ref[:, lanes] + dot_nt3(high_ref[:, lanes], low_ref[:, lanes], state)
        mean = jnp.mean(core * core, axis=-1, keepdims=True)
        gate = 0.5 * gate_ref[:, lanes].astype(F32)
        swish = gate + gate * jnp.tanh(gate)
        hidden = (core * lax.rsqrt(mean + 1e-05) * swish).astype(BF16)
        hid_ref[:, lanes] = hidden
        turned = hidden.astype(F32).T
        low, high = turned[:HALF], turned[HALF:]
        rows = slice(head * HALF, (head + 1) * HALF)
        keep_ref[rows, :] = jnp.where(first, low, high).astype(BF16)
        send_ref[rows, :] = jnp.where(first, high, low)


def gated(where, local, mine, got, gate):
    spec = pl.BlockSpec((TOK, GROUP * DK), lambda h, w: (0, h))
    state = pl.BlockSpec((GROUP, HALF, DK), lambda h, w: (h, 0, 0))
    turned = pl.BlockSpec((GROUP * HALF, TOK), lambda h, w: (h, 0))
    return pl.pallas_call(
        hidden_kernel,
        grid_spec=pltpu.PrefetchScalarGridSpec(
            num_scalar_prefetch=1,
            grid=(H // GROUP,),
            in_specs=[spec, spec, spec, state, state, spec],
            out_specs=[spec, turned, turned],
        ),
        out_shape=[
            jax.ShapeDtypeStruct((TOK, H * DK), BF16),
            jax.ShapeDtypeStruct((H * HALF, TOK), BF16),
            jax.ShapeDtypeStruct((H * HALF, TOK), F32),
        ],
        compiler_params=params(PIECE_LIMIT),
        cost_estimate=cost(6 * TOK * DK * DK * H, 17e6, 2 * TOK * DK * H),
        name="gated_hidden",
    )(where, *local, mine, got, gate)


CHUNK = {"x": (4, 4, 1, 16, TOK), "y": (1, 4, 4, 16, TOK), "z": (4, 1, 4, 16, TOK)}


def product_kernel(axis, steps, where_ref, keep_ref, got_ref, own_ref, other_ref, *refs):
    *outs, token_ref, left_ref, right_ref = refs[-3 - len(steps) :]
    core = where_ref[3]
    token_ref[...] = jnp.zeros_like(token_ref)

    def chunk(ref, j):
        if axis == "y":
            return ref[j]
        if axis == "z":
            return ref[:, j]
        return ref[:, :, j]

    @pl.when(pl.program_id(0) == 0)
    def _():
        me = where_ref[AXES.index(axis)]
        for t, step in enumerate(steps):
            j = lax.rem(me + step(core), 4)
            for part, ref in enumerate((keep_ref, got_ref)):
                lanes = slice(part * TOK, (part + 1) * TOK)
                rows = chunk(ref, j).reshape(256, TOK)
                left_ref[256 * t : 256 * (t + 1), lanes] = rows.astype(BF16)

    right_ref[:TOK, :] = own_ref[...]
    right_ref[TOK:, :] = other_ref[...].astype(BF16)
    total = jnp.dot(left_ref[...], right_ref[...], preferred_element_type=F32)
    for t, out in enumerate(outs):
        out[...] = total[256 * t : 256 * (t + 1)]


BEFORE, OPPOSITE = (lambda core: 3 - 2 * core), (lambda core: 2)
AFTER, MINE = (lambda core: 1 + 2 * core), (lambda core: 0)


def products(axis, steps, where, keep, got, own, other, after):
    blocks = KINDS[axis]
    rows = (256,) * len(steps)
    cotan = pl.BlockSpec((TOK, COLS), lambda i, w: (0, blocks[0] + i))
    whole = pl.BlockSpec((4, 4, 4, 16, TOK), lambda i, w: (0, 0, 0, 0, 0))
    width = COLS * len(blocks)
    return pl.pallas_call(
        functools.partial(product_kernel, axis, steps),
        grid_spec=pltpu.PrefetchScalarGridSpec(
            num_scalar_prefetch=1,
            grid=(len(blocks),),
            in_specs=[whole, whole, cotan, cotan]
            + [pl.BlockSpec(memory_space=pl.ANY)] * len(after),
            out_specs=[pl.BlockSpec((r, COLS), lambda i, w: (0, i)) for r in rows]
            + [pl.BlockSpec((8, DK), lambda i, w: (0, 0))],
            scratch_shapes=[
                pltpu.VMEM((256 * len(steps), 2 * TOK), BF16),
                pltpu.VMEM((2 * TOK, COLS), BF16),
            ],
        ),
        out_shape=[jax.ShapeDtypeStruct((r, width), F32) for r in rows]
        + [jax.ShapeDtypeStruct((8, DK), F32)],
        compiler_params=params(PRODUCT_LIMIT),
        cost_estimate=cost(1e6, 1e6),
        name="products_" + axis,
    )(where, keep, got, own, other, *after)


def relay_kernel(a, b, *rest):
    out, token = rest[-2:]
    out[...] = a[...] + b[...]
    token[...] = jnp.zeros_like(token)


def relay(term, arrived, after):
    rows, width = term.shape
    spec = pl.BlockSpec((rows, COLS), lambda i: (0, i))
    return pl.pallas_call(
        relay_kernel,
        grid=(width // COLS,),
        in_specs=[spec] * 2 + [pl.BlockSpec(memory_space=pl.ANY)] * len(after),
        out_specs=[spec, pl.BlockSpec((8, DK), lambda i: (0, 0))],
        out_shape=[
            jax.ShapeDtypeStruct(term.shape, F32),
            jax.ShapeDtypeStruct((8, DK), F32),
        ],
        input_output_aliases={0: 0},
        compiler_params=params(SMALL_LIMIT),
        cost_estimate=cost(rows * width, 12 * rows * width),
        name="relay",
    )(term, arrived, *after)


def second_kernel(axis, me, where_ref, mine, *rest):
    came, outs, total = rest[:-5], rest[-5:-1], rest[-1]
    core = where_ref[3]
    total[...] = sum((ref[...] for ref in came), mine[...])
    for t in range(4):
        j = lax.rem(where_ref[me] + jnp.where(core == 0, 7 - t, 1 + t), 4)
        if axis == "z":
            for y in range(4):
                row = pl.multiple_of(64 * y + 16 * j, 16)
                outs[t][16 * y : 16 * (y + 1), :] = total[pl.ds(row, 16), :]
        else:
            outs[t][...] = total[pl.ds(pl.multiple_of(64 * j, 64), 64), :]


def add_kernel(where_ref, a, b, out):
    out[...] = a[...] + b[...]


def halves_kernel(me, place, where_ref, a, b, keep, away, total):
    total[...] = a[...] + b[...]
    rows = keep.shape[0]
    row = rows * place(where_ref[me])
    keep[...] = total[pl.ds(pl.multiple_of(row, rows), rows), :]
    away[...] = total[pl.ds(pl.multiple_of(rows - row, rows), rows), :]


def last_kernel(where_ref, *refs):
    out = refs[-1]
    col = 0
    for a, b in zip(refs[0:6:2], refs[1:6:2]):
        width = a.shape[1]
        out[:, col : col + width] = a[...] + b[...]
        col += width


def together(kernels, where, ins, outs, scratch, name):
    def body(where_ref, *refs):
        sets = [[] for _ in kernels]
        at = 0
        for lists in (ins, outs, scratch):
            for mine, part in zip(sets, lists):
                mine += refs[at : at + len(part)]
                at += len(part)
        for kernel, mine in zip(kernels, sets):
            kernel(where_ref, *mine)

    flat = lambda lists: [item for part in lists for item in part]
    results = iter(small_call(body, where, flat(ins), flat(outs), flat(scratch), (), name))
    return [[next(results) for _ in part] for part in outs]


def around(pieces, axis):
    return [pieces[0]] + [send(pieces[d], axis, d) for d in (1, 3, 2)]


def assemble_kernel(where_ref, *refs):
    for ref, d in zip(refs, (0, 1, 3, 2)):
        row = pl.multiple_of(lax.rem(where_ref[0] - d + 4, 4) * 16, 16)
        refs[-1][pl.ds(row, 16), :] = ref[...]


def shards(queries, key_rows, value_rows, log_gate, out_gate, cotangent):
    place = {name: lax.axis_index(name) for name in AXES}
    where = jnp.stack([place[name] for name in AXES]).astype(jnp.int32)
    q, k, v, g = queries[0], key_rows[0], value_rows[0], log_gate[0]
    own = cotangent[0]

    mine, got, local, other = attend(where, q, k, v, g, own)
    hidden, keep, away = gated(where, local, mine, got, out_gate[0])
    theirs = send(away, "c", 1).reshape(4, 4, 4, 16, TOK)
    keep = keep.reshape(4, 4, 4, 16, TOK)

    forward, backward = (lambda c: 1 - 2 * c), (lambda c: 2 * c - 1)
    order = ("x", "y", "z")
    terms, came = {}, {}
    token = ()
    for axis in ("y", "z", "x"):
        first = (BEFORE,) if axis == "x" else (OPPOSITE,)
        term, *token = products(axis, first, where, keep, theirs, own, other, token)
        came[axis] = send(term, axis, forward)
    for axis in ("x", "y", "z"):
        others = (OPPOSITE, AFTER, MINE) if axis == "x" else (BEFORE, AFTER, MINE)
        *terms[axis], t = products(axis, others, where, keep, theirs, own, other, token)
        token = [t]

    def pass_on(axis, n, after):
        term, *after = relay(terms[axis][n], came[axis], after)
        came[axis] = send(term, axis, forward)
        return after

    direct = {axis: (send(terms[axis][0], axis, backward),) for axis in ("y", "z")}
    direct["x"] = ()
    token = pass_on("x", 0, token)
    token = pass_on("y", 1, token)
    token = pass_on("z", 1, token)
    token = pass_on("x", 1, token)

    following = {"x": ("y", "z"), "y": ("z", "x"), "z": ("x", "y")}
    width = {axis: COLS * len(KINDS[axis]) for axis in order}
    parts = together(
        [functools.partial(second_kernel, a, AXES.index(following[a][0])) for a in order],
        where,
        [[terms[a][2], came[a], *direct[a]] for a in order],
        [[(64, width[a])] * 4 for a in order],
        [[(256, width[a])] for a in order],
        "second",
    )
    held = [part[0] for part in parts]
    for step in (1, 2):
        came = [send(h, following[a][0], forward) for h, a in zip(held, order)]
        held = together(
            [add_kernel] * 3,
            where,
            [[part[step], c] for part, c in zip(parts, came)],
            [[(64, width[a])] for a in order],
            [[]] * 3,
            "add",
        )
        held = [h[0] for h in held]
    came = [send(h, following[a][0], forward) for h, a in zip(held, order)]
    pairs = [[part[3], c] for part, c in zip(parts, came)]
    upper, odd = (lambda p: lax.div(p, 2)), (lambda p: lax.rem(p, 2))
    for rows, distance, place_of in ((32, 2, upper), (16, 1, odd)):
        pairs = together(
            [
                functools.partial(halves_kernel, AXES.index(following[a][1]), place_of)
                for a in order
            ],
            where,
            pairs,
            [[(rows, width[a])] * 2 for a in order],
            [[(2 * rows, width[a])] for a in order],
            "halves",
        )
        pairs = [
            [keep, swap(away, following[a][1], distance)]
            for (keep, away), a in zip(pairs, order)
        ]
    rounds = dict(zip(order, pairs))
    (mine,) = small_call(
        last_kernel, where, [r for axis in KINDS for r in rounds[axis]], [(16, D)], name="last"
    )
    pieces = around([mine] * 4, "x")
    weight_grad = pl.pallas_call(
        assemble_kernel,
        in_specs=[pl.BlockSpec(memory_space=pltpu.SMEM)]
        + [pl.BlockSpec(memory_space=pltpu.VMEM)] * len(pieces),
        out_specs=pl.BlockSpec(memory_space=pltpu.VMEM),
        out_shape=jax.ShapeDtypeStruct((64, D), F32),
        compiler_params=pltpu.CompilerParams(vmem_limit_bytes=SMALL_LIMIT),
        cost_estimate=cost(64 * D, 8 * 64 * D),
        name="assemble",
    )(where, *pieces)
    return hidden[None], weight_grad


def solution(mesh):
    fine = Mesh(mesh.devices.reshape(SIZES), AXES)
    rows = P("x", ("y", "z", "c"), None)
    return jax.shard_map(
        shards,
        mesh=fine,
        in_specs=(rows,) * 6,
        out_specs=(rows, P(("y", "z", "c"), None)),
        check_vma=False,
    )
```

```python
import functools

import jax
import jax.numpy as jnp
from jax import lax
from jax.experimental import pallas as pl
from jax.experimental.pallas import tpu as pltpu
from jax.sharding import Mesh, PartitionSpec as P

H = 16
DK = 128
D = 4096
BLOCK = 64
TOK = 512
BLOCKS = TOK // BLOCK
HALF = DK // 2
MSG = HALF + 8
COLS = 512
AXES = ("x", "y", "z", "c")
SIZES = (4, 4, 4, 2)
F32 = jnp.float32
BF16 = jnp.bfloat16
VMEM_LIMIT = 60 * 1024 * 1024
PIECE_LIMIT = 24 * 1024 * 1024
PRODUCT_LIMIT = 28 * 1024 * 1024
SMALL_LIMIT = 16 * 1024 * 1024

KINDS = {"y": (0, 1, 2), "z": (3, 4, 5), "x": (6, 7)}
GROUP = 2


def linear(p):
    return ((p[0] * 4 + p[1]) * 4 + p[2]) * 2 + p[3]


def places():
    return [(x, y, z, c) for x in range(4) for y in range(4) for z in range(4) for c in range(2)]


def shift_pairs(axis, by):
    at = AXES.index(axis)
    pairs = []
    for p in places():
        q = list(p)
        step = by(p[3]) if callable(by) else by
        q[at] = (q[at] + step) % SIZES[at]
        pairs.append((linear(p), linear(q)))
    return pairs


def swap(array, axis, distance):
    at = AXES.index(axis)
    pairs = []
    for p in places():
        q = list(p)
        q[at] ^= distance
        pairs.append((linear(p), linear(q)))
    return lax.ppermute(array, AXES, pairs)


def send(array, axis, by):
    return lax.ppermute(array, AXES, shift_pairs(axis, by))


def params(limit=VMEM_LIMIT):
    return pltpu.CompilerParams(dimension_semantics=("arbitrary",), vmem_limit_bytes=limit)


def cost(flops, nbytes, transcendentals=0):
    return pl.CostEstimate(
        flops=int(flops), bytes_accessed=int(nbytes), transcendentals=int(transcendentals)
    )


def split(a):
    high = a.astype(BF16)
    return high, (a - high.astype(F32)).astype(BF16)


def dot_nt(a, b):
    return lax.dot_general(a, b, (((1,), (1,)), ((), ())), preferred_element_type=F32)


def dot_tn(a, b):
    return lax.dot_general(a, b, (((0,), (0,)), ((), ())), preferred_element_type=F32)


def dot_nt3(ah, al, b):
    n = ah.shape[0]
    high, low = split(b)
    both = dot_nt(jnp.concatenate([ah, al], axis=0), jnp.concatenate([high, low], axis=0))
    m = b.shape[0]
    return both[:n, :m] + (both[:n, m:] + both[n:, :m])


def block_cumsum(g):
    x = g.reshape(TOK // 8, 8, DK)
    row = lax.broadcasted_iota(jnp.int32, x.shape, 1)
    for shift in (1, 2, 4):
        x = x + jnp.where(row >= shift, pltpu.roll(x, shift, 1), 0.0)
    x = x.reshape(BLOCKS, BLOCK // 8, 8, DK)
    parts = []
    run = None
    for i in range(BLOCK // 8):
        part = x[:, i]
        if run is not None:
            part = part + run
        parts.append(part)
        run = part[:, 7:8, :]
    return jnp.stack(parts, axis=1).reshape(BLOCKS, BLOCK, DK), run


def state_kernel(
    where_ref, k_ref, v_ref, g_ref, cotan_ref, keep_ref, send_ref, cum_ref, wide_ref
):
    first = where_ref[3] == 0
    wide_ref[...] = cotan_ref[...].astype(F32)
    for head in range(GROUP):
        lanes = slice(head * DK, (head + 1) * DK)
        cum, end = block_cumsum(g_ref[:, lanes])
        cum_ref[:, lanes] = cum.reshape(TOK, DK)
        k = k_ref[:, lanes].astype(F32).reshape(BLOCKS, BLOCK, DK)
        kend = (k * jnp.exp(end - cum)).astype(BF16)
        decay = jnp.exp(end)
        total = end[0]
        state = None
        for j in range(BLOCKS):
            term = dot_tn(v_ref[j * BLOCK : (j + 1) * BLOCK, lanes], kend[j])
            if j:
                state = state * decay[j] + term
                total = total + end[j]
            else:
                state = term
        row = jnp.broadcast_to(jnp.exp(total), (8, DK))
        low, high = state[:HALF], state[HALF:]
        keep_ref[head, :HALF] = jnp.where(first, low, high)
        send_ref[head, :HALF] = jnp.where(first, high, low)
        keep_ref[head, HALF:] = row
        send_ref[head, HALF:] = row


def local_state(where, k, v, g, cotan):
    out = jax.ShapeDtypeStruct((H, MSG, DK), F32)
    steps = H // GROUP
    heads = pl.BlockSpec((TOK, GROUP * DK), lambda h, w: (0, h))
    wide = pl.BlockSpec((TOK, D // steps), lambda h, w: (0, h))
    return pl.pallas_call(
        state_kernel,
        grid_spec=pltpu.PrefetchScalarGridSpec(
            num_scalar_prefetch=1,
            grid=(steps,),
            in_specs=[heads] * 3 + [wide],
            out_specs=[pl.BlockSpec((GROUP, MSG, DK), lambda h, w: (h, 0, 0))] * 2
            + [heads, wide],
        ),
        out_shape=[out, out]
        + [jax.ShapeDtypeStruct((TOK, n), F32) for n in (H * DK, D)],
        compiler_params=params(PIECE_LIMIT),
        cost_estimate=cost(2 * TOK * DK * DK * H, 26e6, TOK * DK * H),
        name="local_state",
    )(where, k, v, g, cotan)


def core_kernel(q_ref, k_ref, v_ref, cum_ref, *rest):
    out_ref, high_ref, low_ref, token_ref = rest[-4:]
    token_ref[...] = jnp.zeros_like(token_ref)
    shape = (BLOCKS, BLOCK, DK)
    two = 2 * BLOCK
    rows = lax.broadcasted_iota(jnp.int32, (two, two), 0)
    cols = lax.broadcasted_iota(jnp.int32, (two, two), 1)
    mask = (rows >= cols) & ((rows >= BLOCK) == (cols >= BLOCK))
    for head in range(GROUP):
        lanes = slice(head * DK, (head + 1) * DK)
        cum = cum_ref[:, lanes].reshape(shape)
        end = cum[:, BLOCK - 1 : BLOCK, :]
        q = q_ref[:, lanes].astype(F32).reshape(shape)
        k = k_ref[:, lanes].astype(F32).reshape(shape)
        qdec = q * jnp.exp(cum)
        qround = qdec.astype(BF16)
        qrest = (qdec - qround.astype(F32)).astype(BF16)
        decay = jnp.exp(end)
        kfull = k * jnp.exp(-cum)
        kinc = kfull.astype(BF16)
        kend = (kfull * decay).astype(BF16)
        before = jnp.zeros((1, DK), F32)
        state = None
        for pair in range(BLOCKS // 2):
            span = slice(pair * two, (pair + 1) * two)
            qq = qround[2 * pair : 2 * pair + 2].reshape(two, DK)
            kk = kinc[2 * pair : 2 * pair + 2].reshape(two, DK)
            weights = jnp.where(mask, dot_nt(qq, kk), 0.0).astype(BF16)
            intra = jnp.dot(weights, v_ref[span, lanes], preferred_element_type=F32)
            for half in range(2):
                j = 2 * pair + half
                at = slice(j * BLOCK, (j + 1) * BLOCK)
                mine = intra[half * BLOCK : (half + 1) * BLOCK]
                if state is not None:
                    mine = mine + dot_nt3(qround[j], qrest[j], state)
                out_ref[at, lanes] = mine
                far = qdec[j] * jnp.exp(before)
                high, low = split(far)
                high_ref[at, lanes] = high
                low_ref[at, lanes] = low
                before = before + end[j]
                if j < BLOCKS - 1:
                    term = dot_tn(v_ref[at, lanes], kend[j])
                    state = term if state is None else state * decay[j] + term


def local_core(first, steps, q, k, v, cum, after, earlier):
    spec = pl.BlockSpec((TOK, GROUP * DK), lambda h: (0, h + first))
    extra = list(earlier) + [after]
    shape = (TOK, H * DK)
    return pl.pallas_call(
        core_kernel,
        grid=(steps,),
        in_specs=[spec] * 4 + [pl.BlockSpec(memory_space=pl.ANY)] * len(extra),
        out_specs=[spec] * 3 + [pl.BlockSpec((8, DK), lambda h: (0, 0))],
        out_shape=[jax.ShapeDtypeStruct(shape, t) for t in (F32, BF16, BF16)]
        + [jax.ShapeDtypeStruct((8, DK), F32)],
        input_output_aliases={4 + i: i for i in range(len(earlier))},
        compiler_params=params(PIECE_LIMIT),
        cost_estimate=cost(64 * TOK * DK * DK, 20e6, 16 * TOK * DK),
        name="local_core",
    )(q, k, v, cum, *extra)


def chip_kernel(where_ref, keep_ref, got_ref, wide_ref, *outs):
    z, c = where_ref[2], where_ref[3]
    first = c == 0
    for d in range(4):
        base = lax.rem(z + d, 4) * 4
        a = keep_ref[pl.ds(base, 4)]
        b = got_ref[pl.ds(base, 4)]
        early = jnp.where(first, a, b)
        late = jnp.where(first, b, a)
        decay = late[:, HALF : HALF + 1, :]
        outs[d][:, :HALF] = early[:, :HALF] * decay + late[:, :HALF]
        outs[d][:, HALF:] = early[:, HALF:] * late[:, HALF:]


def row_kernel(where_ref, r0, r1, r2, r3, prefix_ref, total_ref, hold):
    z = where_ref[2]
    for d, ref in zip((0, 1, 3, 2), (r0, r1, r2, r3)):
        hold[lax.rem(z - d + 4, 4)] = ref[...]
    state = jnp.zeros((4, HALF, DK), F32)
    decay = jnp.ones((4, 8, DK), F32)
    for i in range(4):
        prefix_ref[i, :, :HALF] = state
        prefix_ref[i, :, HALF:] = decay
        item = hold[i]
        late = item[:, HALF:]
        state = state * late[:, :1, :] + item[:, :HALF]
        decay = decay * late
    total_ref[:, :HALF] = state
    total_ref[:, HALF:] = decay


def back_kernel(where_ref, prefix_ref, r0, r1, r2, r3, *rest):
    outs, hold = rest[:4], rest[4]
    y, z = where_ref[1], where_ref[2]
    for d, ref in zip((0, 1, 3, 2), (r0, r1, r2, r3)):
        hold[lax.rem(y - d + 4, 4)] = ref[...]
    state = jnp.zeros((4, HALF, DK), F32)
    for i in range(3):
        item = hold[i]
        new = state * item[:, HALF : HALF + 1, :] + item[:, :HALF]
        state = jnp.where(i < y, new, state)
    for d in range(4):
        prefix = prefix_ref[lax.rem(z + d, 4)]
        outs[d][...] = state * prefix[:, HALF : HALF + 1, :] + prefix[:, :HALF]


def core_start_kernel(where_ref, keep_ref, got_ref, r0, r1, r2, r3, mine_ref, other_ref):
    z, c = where_ref[2], where_ref[3]
    first = c == 0
    for d, ref in zip((0, 1, 3, 2), (r0, r1, r2, r3)):
        at = pl.ds(lax.rem(z - d + 4, 4) * 4, 4)
        chip = ref[...]
        early = jnp.where(first, keep_ref[at], got_ref[at])
        second = chip * early[:, HALF : HALF + 1, :] + early[:, :HALF]
        mine_ref[at] = jnp.where(first, chip, second)
        other_ref[at] = jnp.where(first, second, chip)


def small_call(kernel, where, arrays, outs, scratch=(), after=(), name=None):
    whole = [pl.BlockSpec(memory_space=pltpu.VMEM)]
    nbytes = sum(a.size * 4 for a in arrays)
    used = 1 + len(arrays)

    def body(*refs):
        kernel(*refs[:used], *refs[used + len(after) :])

    return pl.pallas_call(
        body,
        in_specs=[pl.BlockSpec(memory_space=pltpu.SMEM)]
        + whole * len(arrays)
        + [pl.BlockSpec(memory_space=pl.ANY)] * len(after),
        out_specs=whole * len(outs),
        out_shape=[jax.ShapeDtypeStruct(s, F32) for s in outs],
        scratch_shapes=[pltpu.VMEM(s, F32) for s in scratch],
        compiler_params=pltpu.CompilerParams(vmem_limit_bytes=SMALL_LIMIT),
        cost_estimate=cost(nbytes, 2 * nbytes),
        name=name,
    )(where, *arrays, *after)


def chip_total(where, keep, got, wide):
    vmem = pl.BlockSpec(memory_space=pltpu.VMEM)
    away = pl.BlockSpec(memory_space=pl.ANY)
    return pl.pallas_call(
        chip_kernel,
        in_specs=[pl.BlockSpec(memory_space=pltpu.SMEM), vmem, vmem, away],
        out_specs=[vmem] * 4 + [away],
        out_shape=[jax.ShapeDtypeStruct((4, MSG, DK), F32)] * 4
        + [jax.ShapeDtypeStruct(wide.shape, F32)],
        input_output_aliases={3: 4},
        compiler_params=pltpu.CompilerParams(vmem_limit_bytes=SMALL_LIMIT),
        cost_estimate=cost(H * MSG * DK * 4, 16 * H * MSG * DK),
        name="chip_total",
    )(where, keep, got, wide)


def attend(where, q, k, v, g, own):
    keep, away, cum, wide = local_state(where, k, v, g, own)
    got = send(away, "c", 1)
    msg = (4, MSG, DK)
    *parts, wide = chip_total(where, keep, got, wide)
    other = send(wide, "c", 1)
    arrived = around(parts, "z")
    *local, token = local_core(0, 3, q, k, v, cum, parts[1], ())
    prefix, total = small_call(
        row_kernel, where, arrived, [(4,) + msg, msg], [(4,) + msg], [token], "row_total"
    )
    rows = around([total] * 4, "y")
    *local, token = local_core(3, 2, q, k, v, cum, total, local)
    out = (4, HALF, DK)
    back = small_call(
        back_kernel, where, [prefix] + rows, [out] * 4, [(4,) + msg], [token], "row_start"
    )
    arrived = around(back, "z")
    *local, token = local_core(5, 2, q, k, v, cum, back[1], local)
    mine, theirs = small_call(
        core_start_kernel,
        where,
        [keep, got] + arrived,
        [(H, HALF, DK)] * 2,
        after=[token],
        name="core_start",
    )
    *local, token = local_core(7, 1, q, k, v, cum, theirs, local)
    return mine, send(theirs, "c", 1), local, other


def hidden_kernel(
    where_ref, out_ref, high_ref, low_ref, mine_ref, got_ref, gate_ref, hid_ref, keep_ref, send_ref
):
    first = where_ref[3] == 0
    for head in range(GROUP):
        lanes = slice(head * DK, (head + 1) * DK)
        a, b = mine_ref[head], got_ref[head]
        state = jnp.concatenate([jnp.where(first, a, b), jnp.where(first, b, a)], axis=0)
        core = out_ref[:, lanes] + dot_nt3(high_ref[:, lanes], low_ref[:, lanes], state)
        mean = jnp.mean(core * core, axis=-1, keepdims=True)
        gate = 0.5 * gate_ref[:, lanes].astype(F32)
        swish = gate + gate * jnp.tanh(gate)
        hidden = (core * lax.rsqrt(mean + 1e-05) * swish).astype(BF16)
        hid_ref[:, lanes] = hidden
        turned = hidden.astype(F32).T
        low, high = turned[:HALF], turned[HALF:]
        rows = slice(head * HALF, (head + 1) * HALF)
        keep_ref[rows, :] = jnp.where(first, low, high).astype(BF16)
        send_ref[rows, :] = jnp.where(first, high, low)


def gated(where, local, mine, got, gate):
    spec = pl.BlockSpec((TOK, GROUP * DK), lambda h, w: (0, h))
    state = pl.BlockSpec((GROUP, HALF, DK), lambda h, w: (h, 0, 0))
    turned = pl.BlockSpec((GROUP * HALF, TOK), lambda h, w: (h, 0))
    return pl.pallas_call(
        hidden_kernel,
        grid_spec=pltpu.PrefetchScalarGridSpec(
            num_scalar_prefetch=1,
            grid=(H // GROUP,),
            in_specs=[spec, spec, spec, state, state, spec],
            out_specs=[spec, turned, turned],
        ),
        out_shape=[
            jax.ShapeDtypeStruct((TOK, H * DK), BF16),
            jax.ShapeDtypeStruct((H * HALF, TOK), BF16),
            jax.ShapeDtypeStruct((H * HALF, TOK), F32),
        ],
        compiler_params=params(PIECE_LIMIT),
        cost_estimate=cost(6 * TOK * DK * DK * H, 17e6, 2 * TOK * DK * H),
        name="gated_hidden",
    )(where, *local, mine, got, gate)


CHUNK = {"x": (4, 4, 1, 16, TOK), "y": (1, 4, 4, 16, TOK), "z": (4, 1, 4, 16, TOK)}


def product_kernel(axis, steps, where_ref, keep_ref, got_ref, own_ref, other_ref, *refs):
    *outs, token_ref, left_ref, right_ref = refs[-3 - len(steps) :]
    core = where_ref[3]
    token_ref[...] = jnp.zeros_like(token_ref)

    def chunk(ref, j):
        if axis == "y":
            return ref[j]
        if axis == "z":
            return ref[:, j]
        return ref[:, :, j]

    @pl.when(pl.program_id(0) == 0)
    def _():
        me = where_ref[AXES.index(axis)]
        for t, step in enumerate(steps):
            j = lax.rem(me + step(core), 4)
            for part, ref in enumerate((keep_ref, got_ref)):
                lanes = slice(part * TOK, (part + 1) * TOK)
                rows = chunk(ref, j).reshape(256, TOK)
                left_ref[256 * t : 256 * (t + 1), lanes] = rows.astype(BF16)

    right_ref[:TOK, :] = own_ref[...]
    right_ref[TOK:, :] = other_ref[...].astype(BF16)
    total = jnp.dot(left_ref[...], right_ref[...], preferred_element_type=F32)
    for t, out in enumerate(outs):
        out[...] = total[256 * t : 256 * (t + 1)]


BEFORE, OPPOSITE = (lambda core: 3 - 2 * core), (lambda core: 2)
AFTER, MINE = (lambda core: 1 + 2 * core), (lambda core: 0)


def products(axis, steps, where, keep, got, own, other, after):
    blocks = KINDS[axis]
    rows = (256,) * len(steps)
    cotan = pl.BlockSpec((TOK, COLS), lambda i, w: (0, blocks[0] + i))
    whole = pl.BlockSpec((4, 4, 4, 16, TOK), lambda i, w: (0, 0, 0, 0, 0))
    width = COLS * len(blocks)
    return pl.pallas_call(
        functools.partial(product_kernel, axis, steps),
        grid_spec=pltpu.PrefetchScalarGridSpec(
            num_scalar_prefetch=1,
            grid=(len(blocks),),
            in_specs=[whole, whole, cotan, cotan]
            + [pl.BlockSpec(memory_space=pl.ANY)] * len(after),
            out_specs=[pl.BlockSpec((r, COLS), lambda i, w: (0, i)) for r in rows]
            + [pl.BlockSpec((8, DK), lambda i, w: (0, 0))],
            scratch_shapes=[
                pltpu.VMEM((256 * len(steps), 2 * TOK), BF16),
                pltpu.VMEM((2 * TOK, COLS), BF16),
            ],
        ),
        out_shape=[jax.ShapeDtypeStruct((r, width), F32) for r in rows]
        + [jax.ShapeDtypeStruct((8, DK), F32)],
        compiler_params=params(PRODUCT_LIMIT),
        cost_estimate=cost(1e6, 1e6),
        name="products_" + axis,
    )(where, keep, got, own, other, *after)


def relay_kernel(a, b, *rest):
    out, token = rest[-2:]
    out[...] = a[...] + b[...]
    token[...] = jnp.zeros_like(token)


def relay(term, arrived, after):
    rows, width = term.shape
    spec = pl.BlockSpec((rows, COLS), lambda i: (0, i))
    return pl.pallas_call(
        relay_kernel,
        grid=(width // COLS,),
        in_specs=[spec] * 2 + [pl.BlockSpec(memory_space=pl.ANY)] * len(after),
        out_specs=[spec, pl.BlockSpec((8, DK), lambda i: (0, 0))],
        out_shape=[
            jax.ShapeDtypeStruct(term.shape, F32),
            jax.ShapeDtypeStruct((8, DK), F32),
        ],
        input_output_aliases={0: 0},
        compiler_params=params(SMALL_LIMIT),
        cost_estimate=cost(rows * width, 12 * rows * width),
        name="relay",
    )(term, arrived, *after)


def second_kernel(axis, me, where_ref, mine, *rest):
    came, outs, total = rest[:-5], rest[-5:-1], rest[-1]
    core = where_ref[3]
    total[...] = sum((ref[...] for ref in came), mine[...])
    for t in range(4):
        step = (OPPOSITE, BEFORE, AFTER, MINE)[t]
        j = lax.rem(where_ref[me] + step(core), 4)
        if axis == "z":
            for y in range(4):
                row = pl.multiple_of(64 * y + 16 * j, 16)
                outs[t][16 * y : 16 * (y + 1), :] = total[pl.ds(row, 16), :]
        else:
            outs[t][...] = total[pl.ds(pl.multiple_of(64 * j, 64), 64), :]


def pass_kernel(where_ref, forth, came, *rest):
    rest[-2][...] = forth[...] + came[...]
    rest[-1][...] = sum((ref[...] for ref in rest[1:-2]), rest[0][...])


def halves_kernel(me, place, where_ref, a, *rest):
    came, (keep, away, total) = rest[:-3], rest[-3:]
    total[...] = sum((ref[...] for ref in came), a[...])
    rows = keep.shape[0]
    row = rows * place(where_ref[me])
    keep[...] = total[pl.ds(pl.multiple_of(row, rows), rows), :]
    away[...] = total[pl.ds(pl.multiple_of(rows - row, rows), rows), :]


def last_kernel(where_ref, *refs):
    out = refs[-1]
    col = 0
    for a, b in zip(refs[0:6:2], refs[1:6:2]):
        width = a.shape[1]
        out[:, col : col + width] = a[...] + b[...]
        col += width


def together(kernels, where, ins, outs, scratch, name):
    def body(where_ref, *refs):
        sets = [[] for _ in kernels]
        at = 0
        for lists in (ins, outs, scratch):
            for mine, part in zip(sets, lists):
                mine += refs[at : at + len(part)]
                at += len(part)
        for kernel, mine in zip(kernels, sets):
            kernel(where_ref, *mine)

    flat = lambda lists: [item for part in lists for item in part]
    results = iter(small_call(body, where, flat(ins), flat(outs), flat(scratch), (), name))
    return [[next(results) for _ in part] for part in outs]


def around(pieces, axis):
    return [pieces[0]] + [send(pieces[d], axis, d) for d in (1, 3, 2)]


def assemble_kernel(where_ref, *refs):
    for ref, d in zip(refs, (0, 1, 3, 2)):
        row = pl.multiple_of(lax.rem(where_ref[0] - d + 4, 4) * 16, 16)
        refs[-1][pl.ds(row, 16), :] = ref[...]


def shards(queries, key_rows, value_rows, log_gate, out_gate, cotangent):
    place = {name: lax.axis_index(name) for name in AXES}
    where = jnp.stack([place[name] for name in AXES]).astype(jnp.int32)
    q, k, v, g = queries[0], key_rows[0], value_rows[0], log_gate[0]
    own = cotangent[0]

    mine, got, local, other = attend(where, q, k, v, g, own)
    hidden, keep, away = gated(where, local, mine, got, out_gate[0])
    theirs = send(away, "c", 1).reshape(4, 4, 4, 16, TOK)
    keep = keep.reshape(4, 4, 4, 16, TOK)

    forward, backward = (lambda c: 1 - 2 * c), (lambda c: 2 * c - 1)
    order = ("x", "y", "z")
    terms, came = {}, {}
    token = ()
    for axis in ("y", "z", "x"):
        first = (BEFORE,) if axis == "x" else (OPPOSITE,)
        term, *token = products(axis, first, where, keep, theirs, own, other, token)
        came[axis] = send(term, axis, forward)
    for axis in ("x", "y", "z"):
        others = (OPPOSITE, AFTER, MINE) if axis == "x" else (BEFORE, AFTER, MINE)
        *terms[axis], t = products(axis, others, where, keep, theirs, own, other, token)
        token = [t]

    def pass_on(axis, n, after):
        term, *after = relay(terms[axis][n], came[axis], after)
        came[axis] = send(term, axis, forward)
        return after

    direct = {axis: (send(terms[axis][0], axis, backward),) for axis in ("y", "z")}
    direct["x"] = ()
    token = pass_on("x", 0, token)
    token = pass_on("y", 1, token)
    token = pass_on("z", 1, token)
    token = pass_on("x", 1, token)

    following = {"x": ("y", "z"), "y": ("z", "x"), "z": ("x", "y")}
    width = {axis: COLS * len(KINDS[axis]) for axis in order}
    parts = together(
        [functools.partial(second_kernel, a, AXES.index(following[a][0])) for a in order],
        where,
        [[terms[a][2], came[a], *direct[a]] for a in order],
        [[(64, width[a])] * 4 for a in order],
        [[(256, width[a])] for a in order],
        "second",
    )
    parts = dict(zip(order, parts))
    came = {a: send(parts[a][0], following[a][0], forward) for a in ("y", "z", "x")}
    straight = {a: [send(parts[a][1], following[a][0], backward)] for a in ("y", "z")}
    passed = together(
        [pass_kernel] * 3,
        where,
        [
            [parts[a][2], came[a]] + ([parts[a][3]] + straight[a] if a != "x" else [parts[a][1]])
            for a in order
        ],
        [[(64, width[a])] * 2 for a in order],
        [[]] * 3,
        "pass_on",
    )
    pairs = []
    for (forth, mine), a in zip(passed, order):
        arrived = [send(forth, following[a][0], forward)]
        if a == "x":
            mine, arrived = parts[a][3], arrived + [send(mine, following[a][0], backward)]
        pairs.append([mine] + arrived)
    upper, odd = (lambda p: lax.div(p, 2)), (lambda p: lax.rem(p, 2))
    for rows, distance, place_of in ((32, 2, upper), (16, 1, odd)):
        pairs = together(
            [
                functools.partial(halves_kernel, AXES.index(following[a][1]), place_of)
                for a in order
            ],
            where,
            pairs,
            [[(rows, width[a])] * 2 for a in order],
            [[(2 * rows, width[a])] for a in order],
            "halves",
        )
        pairs = [
            [keep, swap(away, following[a][1], distance)]
            for (keep, away), a in zip(pairs, order)
        ]
    rounds = dict(zip(order, pairs))
    (mine,) = small_call(
        last_kernel, where, [r for axis in KINDS for r in rounds[axis]], [(16, D)], name="last"
    )
    pieces = around([mine] * 4, "x")
    weight_grad = pl.pallas_call(
        assemble_kernel,
        in_specs=[pl.BlockSpec(memory_space=pltpu.SMEM)]
        + [pl.BlockSpec(memory_space=pltpu.VMEM)] * len(pieces),
        out_specs=pl.BlockSpec(memory_space=pltpu.VMEM),
        out_shape=jax.ShapeDtypeStruct((64, D), F32),
        compiler_params=pltpu.CompilerParams(vmem_limit_bytes=SMALL_LIMIT),
        cost_estimate=cost(64 * D, 8 * 64 * D),
        name="assemble",
    )(where, *pieces)
    return hidden[None], weight_grad


def solution(mesh):
    fine = Mesh(mesh.devices.reshape(SIZES), AXES)
    rows = P("x", ("y", "z", "c"), None)
    return jax.shard_map(
        shards,
        mesh=fine,
        in_specs=(rows,) * 6,
        out_specs=(rows, P(("y", "z", "c"), None)),
        check_vma=False,
    )
```

```python
import functools

import jax
import jax.numpy as jnp
from jax import lax
from jax.experimental import pallas as pl
from jax.experimental.pallas import tpu as pltpu
from jax.sharding import Mesh, PartitionSpec as P

H = 16
DK = 128
D = 4096
BLOCK = 64
TOK = 512
BLOCKS = TOK // BLOCK
HALF = DK // 2
MSG = HALF + 8
COLS = 512
AXES = ("x", "y", "z", "c")
SIZES = (4, 4, 4, 2)
F32 = jnp.float32
BF16 = jnp.bfloat16
VMEM_LIMIT = 60 * 1024 * 1024
PIECE_LIMIT = 24 * 1024 * 1024
PRODUCT_LIMIT = 28 * 1024 * 1024
SMALL_LIMIT = 16 * 1024 * 1024

KINDS = {"y": (0, 1, 2), "z": (3, 4, 5), "x": (6, 7)}
GROUP = 2
LARGE = 4


def linear(p):
    return ((p[0] * 4 + p[1]) * 4 + p[2]) * 2 + p[3]


def places():
    return [(x, y, z, c) for x in range(4) for y in range(4) for z in range(4) for c in range(2)]


def shift_pairs(axis, by):
    at = AXES.index(axis)
    pairs = []
    for p in places():
        q = list(p)
        step = by(p[3]) if callable(by) else by
        q[at] = (q[at] + step) % SIZES[at]
        pairs.append((linear(p), linear(q)))
    return pairs


def swap(array, axis, distance):
    at = AXES.index(axis)
    pairs = []
    for p in places():
        q = list(p)
        q[at] ^= distance
        pairs.append((linear(p), linear(q)))
    return lax.ppermute(array, AXES, pairs)


def send(array, axis, by):
    return lax.ppermute(array, AXES, shift_pairs(axis, by))


def params(limit=VMEM_LIMIT):
    return pltpu.CompilerParams(dimension_semantics=("arbitrary",), vmem_limit_bytes=limit)


def cost(flops, nbytes, transcendentals=0):
    return pl.CostEstimate(
        flops=int(flops), bytes_accessed=int(nbytes), transcendentals=int(transcendentals)
    )


def split(a):
    high = a.astype(BF16)
    return high, (a - high.astype(F32)).astype(BF16)


def dot_nt(a, b):
    return lax.dot_general(a, b, (((1,), (1,)), ((), ())), preferred_element_type=F32)


def dot_tn(a, b):
    return lax.dot_general(a, b, (((0,), (0,)), ((), ())), preferred_element_type=F32)


def dot_nt3(ah, al, b):
    n = ah.shape[0]
    high, low = split(b)
    both = dot_nt(jnp.concatenate([ah, al], axis=0), jnp.concatenate([high, low], axis=0))
    m = b.shape[0]
    return both[:n, :m] + (both[:n, m:] + both[n:, :m])


def block_cumsum(g):
    x = g.reshape(TOK // 8, 8, DK)
    row = lax.broadcasted_iota(jnp.int32, x.shape, 1)
    for shift in (1, 2, 4):
        x = x + jnp.where(row >= shift, pltpu.roll(x, shift, 1), 0.0)
    x = x.reshape(BLOCKS, BLOCK // 8, 8, DK)
    parts = []
    run = None
    for i in range(BLOCK // 8):
        part = x[:, i]
        if run is not None:
            part = part + run
        parts.append(part)
        run = part[:, 7:8, :]
    return jnp.stack(parts, axis=1).reshape(BLOCKS, BLOCK, DK), run


def state_kernel(
    where_ref, k_ref, v_ref, g_ref, cotan_ref, keep_ref, send_ref, cum_ref, wide_ref
):
    first = where_ref[3] == 0
    wide_ref[...] = cotan_ref[...].astype(F32)
    for head in range(LARGE):
        lanes = slice(head * DK, (head + 1) * DK)
        cum, end = block_cumsum(g_ref[:, lanes])
        cum_ref[:, lanes] = cum.reshape(TOK, DK)
        k = k_ref[:, lanes].astype(F32).reshape(BLOCKS, BLOCK, DK)
        kend = (k * jnp.exp(end - cum)).astype(BF16)
        decay = jnp.exp(end)
        total = end[0]
        state = None
        for j in range(BLOCKS):
            term = dot_tn(v_ref[j * BLOCK : (j + 1) * BLOCK, lanes], kend[j])
            if j:
                state = state * decay[j] + term
                total = total + end[j]
            else:
                state = term
        row = jnp.broadcast_to(jnp.exp(total), (8, DK))
        low, high = state[:HALF], state[HALF:]
        keep_ref[head, :HALF] = jnp.where(first, low, high)
        send_ref[head, :HALF] = jnp.where(first, high, low)
        keep_ref[head, HALF:] = row
        send_ref[head, HALF:] = row


def local_state(where, k, v, g, cotan):
    out = jax.ShapeDtypeStruct((H, MSG, DK), F32)
    steps = H // LARGE
    heads = pl.BlockSpec((TOK, LARGE * DK), lambda h, w: (0, h))
    wide = pl.BlockSpec((TOK, D // steps), lambda h, w: (0, h))
    return pl.pallas_call(
        state_kernel,
        grid_spec=pltpu.PrefetchScalarGridSpec(
            num_scalar_prefetch=1,
            grid=(steps,),
            in_specs=[heads] * 3 + [wide],
            out_specs=[pl.BlockSpec((LARGE, MSG, DK), lambda h, w: (h, 0, 0))] * 2
            + [heads, wide],
        ),
        out_shape=[out, out]
        + [jax.ShapeDtypeStruct((TOK, n), F32) for n in (H * DK, D)],
        compiler_params=params(PIECE_LIMIT),
        cost_estimate=cost(2 * TOK * DK * DK * H, 26e6, TOK * DK * H),
        name="local_state",
    )(where, k, v, g, cotan)


def core_kernel(q_ref, k_ref, v_ref, cum_ref, *rest):
    out_ref, high_ref, low_ref, token_ref = rest[-4:]
    token_ref[...] = jnp.zeros_like(token_ref)
    shape = (BLOCKS, BLOCK, DK)
    two = 2 * BLOCK
    rows = lax.broadcasted_iota(jnp.int32, (two, two), 0)
    cols = lax.broadcasted_iota(jnp.int32, (two, two), 1)
    mask = (rows >= cols) & ((rows >= BLOCK) == (cols >= BLOCK))
    for head in range(GROUP):
        lanes = slice(head * DK, (head + 1) * DK)
        cum = cum_ref[:, lanes].reshape(shape)
        end = cum[:, BLOCK - 1 : BLOCK, :]
        q = q_ref[:, lanes].astype(F32).reshape(shape)
        k = k_ref[:, lanes].astype(F32).reshape(shape)
        qdec = q * jnp.exp(cum)
        qround = qdec.astype(BF16)
        qrest = (qdec - qround.astype(F32)).astype(BF16)
        decay = jnp.exp(end)
        kfull = k * jnp.exp(-cum)
        kinc = kfull.astype(BF16)
        kend = (kfull * decay).astype(BF16)
        before = jnp.zeros((1, DK), F32)
        state = None
        for pair in range(BLOCKS // 2):
            span = slice(pair * two, (pair + 1) * two)
            qq = qround[2 * pair : 2 * pair + 2].reshape(two, DK)
            kk = kinc[2 * pair : 2 * pair + 2].reshape(two, DK)
            weights = jnp.where(mask, dot_nt(qq, kk), 0.0).astype(BF16)
            intra = jnp.dot(weights, v_ref[span, lanes], preferred_element_type=F32)
            for half in range(2):
                j = 2 * pair + half
                at = slice(j * BLOCK, (j + 1) * BLOCK)
                mine = intra[half * BLOCK : (half + 1) * BLOCK]
                if state is not None:
                    mine = mine + dot_nt3(qround[j], qrest[j], state)
                out_ref[at, lanes] = mine
                far = qdec[j] * jnp.exp(before)
                high, low = split(far)
                high_ref[at, lanes] = high
                low_ref[at, lanes] = low
                before = before + end[j]
                if j < BLOCKS - 1:
                    term = dot_tn(v_ref[at, lanes], kend[j])
                    state = term if state is None else state * decay[j] + term


def local_core(first, steps, q, k, v, cum, after, earlier):
    spec = pl.BlockSpec((TOK, GROUP * DK), lambda h: (0, h + first))
    extra = list(earlier) + [after]
    shape = (TOK, H * DK)
    return pl.pallas_call(
        core_kernel,
        grid=(steps,),
        in_specs=[spec] * 4 + [pl.BlockSpec(memory_space=pl.ANY)] * len(extra),
        out_specs=[spec] * 3 + [pl.BlockSpec((8, DK), lambda h: (0, 0))],
        out_shape=[jax.ShapeDtypeStruct(shape, t) for t in (F32, BF16, BF16)]
        + [jax.ShapeDtypeStruct((8, DK), F32)],
        input_output_aliases={4 + i: i for i in range(len(earlier))},
        compiler_params=params(PIECE_LIMIT),
        cost_estimate=cost(64 * TOK * DK * DK, 20e6, 16 * TOK * DK),
        name="local_core",
    )(q, k, v, cum, *extra)


def chip_kernel(where_ref, keep_ref, got_ref, wide_ref, *outs):
    z, c = where_ref[2], where_ref[3]
    first = c == 0
    for d in range(4):
        base = lax.rem(z + d, 4) * 4
        a = keep_ref[pl.ds(base, 4)]
        b = got_ref[pl.ds(base, 4)]
        early = jnp.where(first, a, b)
        late = jnp.where(first, b, a)
        decay = late[:, HALF : HALF + 1, :]
        outs[d][:, :HALF] = early[:, :HALF] * decay + late[:, :HALF]
        outs[d][:, HALF:] = early[:, HALF:] * late[:, HALF:]


def row_kernel(where_ref, r0, r1, r2, r3, prefix_ref, total_ref, hold):
    z = where_ref[2]
    for d, ref in zip((0, 1, 3, 2), (r0, r1, r2, r3)):
        hold[lax.rem(z - d + 4, 4)] = ref[...]
    state = jnp.zeros((4, HALF, DK), F32)
    decay = jnp.ones((4, 8, DK), F32)
    for i in range(4):
        prefix_ref[i, :, :HALF] = state
        prefix_ref[i, :, HALF:] = decay
        item = hold[i]
        late = item[:, HALF:]
        state = state * late[:, :1, :] + item[:, :HALF]
        decay = decay * late
    total_ref[:, :HALF] = state
    total_ref[:, HALF:] = decay


def back_kernel(where_ref, prefix_ref, r0, r1, r2, r3, *rest):
    outs, hold = rest[:4], rest[4]
    y, z = where_ref[1], where_ref[2]
    for d, ref in zip((0, 1, 3, 2), (r0, r1, r2, r3)):
        hold[lax.rem(y - d + 4, 4)] = ref[...]
    state = jnp.zeros((4, HALF, DK), F32)
    for i in range(3):
        item = hold[i]
        new = state * item[:, HALF : HALF + 1, :] + item[:, :HALF]
        state = jnp.where(i < y, new, state)
    for d in range(4):
        prefix = prefix_ref[lax.rem(z + d, 4)]
        outs[d][...] = state * prefix[:, HALF : HALF + 1, :] + prefix[:, :HALF]


def core_start_kernel(where_ref, keep_ref, got_ref, r0, r1, r2, r3, mine_ref, other_ref):
    z, c = where_ref[2], where_ref[3]
    first = c == 0
    for d, ref in zip((0, 1, 3, 2), (r0, r1, r2, r3)):
        at = pl.ds(lax.rem(z - d + 4, 4) * 4, 4)
        chip = ref[...]
        early = jnp.where(first, keep_ref[at], got_ref[at])
        second = chip * early[:, HALF : HALF + 1, :] + early[:, :HALF]
        mine_ref[at] = jnp.where(first, chip, second)
        other_ref[at] = jnp.where(first, second, chip)


def small_call(kernel, where, arrays, outs, scratch=(), after=(), name=None):
    whole = [pl.BlockSpec(memory_space=pltpu.VMEM)]
    nbytes = sum(a.size * 4 for a in arrays)
    used = 1 + len(arrays)

    def body(*refs):
        kernel(*refs[:used], *refs[used + len(after) :])

    return pl.pallas_call(
        body,
        in_specs=[pl.BlockSpec(memory_space=pltpu.SMEM)]
        + whole * len(arrays)
        + [pl.BlockSpec(memory_space=pl.ANY)] * len(after),
        out_specs=whole * len(outs),
        out_shape=[jax.ShapeDtypeStruct(s, F32) for s in outs],
        scratch_shapes=[pltpu.VMEM(s, F32) for s in scratch],
        compiler_params=pltpu.CompilerParams(vmem_limit_bytes=SMALL_LIMIT),
        cost_estimate=cost(nbytes, 2 * nbytes),
        name=name,
    )(where, *arrays, *after)


def chip_total(where, keep, got, wide):
    vmem = pl.BlockSpec(memory_space=pltpu.VMEM)
    away = pl.BlockSpec(memory_space=pl.ANY)
    return pl.pallas_call(
        chip_kernel,
        in_specs=[pl.BlockSpec(memory_space=pltpu.SMEM), vmem, vmem, away],
        out_specs=[vmem] * 4 + [away],
        out_shape=[jax.ShapeDtypeStruct((4, MSG, DK), F32)] * 4
        + [jax.ShapeDtypeStruct(wide.shape, F32)],
        input_output_aliases={3: 4},
        compiler_params=pltpu.CompilerParams(vmem_limit_bytes=SMALL_LIMIT),
        cost_estimate=cost(H * MSG * DK * 4, 16 * H * MSG * DK),
        name="chip_total",
    )(where, keep, got, wide)


def attend(where, q, k, v, g, own):
    keep, away, cum, wide = local_state(where, k, v, g, own)
    got = send(away, "c", 1)
    msg = (4, MSG, DK)
    *parts, wide = chip_total(where, keep, got, wide)
    other = send(wide, "c", 1)
    arrived = around(parts, "z")
    *local, token = local_core(0, 3, q, k, v, cum, parts[1], ())
    prefix, total = small_call(
        row_kernel, where, arrived, [(4,) + msg, msg], [(4,) + msg], [token], "row_total"
    )
    rows = around([total] * 4, "y")
    *local, token = local_core(3, 2, q, k, v, cum, total, local)
    out = (4, HALF, DK)
    back = small_call(
        back_kernel, where, [prefix] + rows, [out] * 4, [(4,) + msg], [token], "row_start"
    )
    arrived = around(back, "z")
    *local, token = local_core(5, 2, q, k, v, cum, back[1], local)
    mine, theirs = small_call(
        core_start_kernel,
        where,
        [keep, got] + arrived,
        [(H, HALF, DK)] * 2,
        after=[token],
        name="core_start",
    )
    *local, token = local_core(7, 1, q, k, v, cum, theirs, local)
    return mine, send(theirs, "c", 1), local, other


def hidden_kernel(
    where_ref, out_ref, high_ref, low_ref, mine_ref, got_ref, gate_ref, hid_ref, keep_ref, send_ref
):
    first = where_ref[3] == 0
    for head in range(LARGE):
        lanes = slice(head * DK, (head + 1) * DK)
        a, b = mine_ref[head], got_ref[head]
        state = jnp.concatenate([jnp.where(first, a, b), jnp.where(first, b, a)], axis=0)
        core = out_ref[:, lanes] + dot_nt3(high_ref[:, lanes], low_ref[:, lanes], state)
        mean = jnp.mean(core * core, axis=-1, keepdims=True)
        gate = 0.5 * gate_ref[:, lanes].astype(F32)
        swish = gate + gate * jnp.tanh(gate)
        hidden = (core * lax.rsqrt(mean + 1e-05) * swish).astype(BF16)
        hid_ref[:, lanes] = hidden
        turned = hidden.astype(F32).T
        low, high = turned[:HALF], turned[HALF:]
        rows = slice(head * HALF, (head + 1) * HALF)
        keep_ref[rows, :] = jnp.where(first, low, high).astype(BF16)
        send_ref[rows, :] = jnp.where(first, high, low)


def gated(where, local, mine, got, gate):
    spec = pl.BlockSpec((TOK, LARGE * DK), lambda h, w: (0, h))
    state = pl.BlockSpec((LARGE, HALF, DK), lambda h, w: (h, 0, 0))
    turned = pl.BlockSpec((LARGE * HALF, TOK), lambda h, w: (h, 0))
    return pl.pallas_call(
        hidden_kernel,
        grid_spec=pltpu.PrefetchScalarGridSpec(
            num_scalar_prefetch=1,
            grid=(H // LARGE,),
            in_specs=[spec, spec, spec, state, state, spec],
            out_specs=[spec, turned, turned],
        ),
        out_shape=[
            jax.ShapeDtypeStruct((TOK, H * DK), BF16),
            jax.ShapeDtypeStruct((H * HALF, TOK), BF16),
            jax.ShapeDtypeStruct((H * HALF, TOK), F32),
        ],
        compiler_params=params(PIECE_LIMIT),
        cost_estimate=cost(6 * TOK * DK * DK * H, 17e6, 2 * TOK * DK * H),
        name="gated_hidden",
    )(where, *local, mine, got, gate)


CHUNK = {"x": (4, 4, 1, 16, TOK), "y": (1, 4, 4, 16, TOK), "z": (4, 1, 4, 16, TOK)}


def product_kernel(axis, steps, where_ref, keep_ref, got_ref, own_ref, other_ref, *refs):
    *outs, token_ref, left_ref, right_ref = refs[-3 - len(steps) :]
    core = where_ref[3]
    token_ref[...] = jnp.zeros_like(token_ref)

    def chunk(ref, j):
        if axis == "y":
            return ref[j]
        if axis == "z":
            return ref[:, j]
        return ref[:, :, j]

    @pl.when(pl.program_id(0) == 0)
    def _():
        me = where_ref[AXES.index(axis)]
        for t, step in enumerate(steps):
            j = lax.rem(me + step(core), 4)
            for part, ref in enumerate((keep_ref, got_ref)):
                lanes = slice(part * TOK, (part + 1) * TOK)
                rows = chunk(ref, j).reshape(256, TOK)
                left_ref[256 * t : 256 * (t + 1), lanes] = rows.astype(BF16)

    right_ref[:TOK, :] = own_ref[...]
    right_ref[TOK:, :] = other_ref[...].astype(BF16)
    total = jnp.dot(left_ref[...], right_ref[...], preferred_element_type=F32)
    for t, out in enumerate(outs):
        out[...] = total[256 * t : 256 * (t + 1)]


BEFORE, OPPOSITE = (lambda core: 3 - 2 * core), (lambda core: 2)
AFTER, MINE = (lambda core: 1 + 2 * core), (lambda core: 0)


def products(axis, steps, where, keep, got, own, other, after):
    blocks = KINDS[axis]
    rows = (256,) * len(steps)
    cotan = pl.BlockSpec((TOK, COLS), lambda i, w: (0, blocks[0] + i))
    whole = pl.BlockSpec((4, 4, 4, 16, TOK), lambda i, w: (0, 0, 0, 0, 0))
    width = COLS * len(blocks)
    return pl.pallas_call(
        functools.partial(product_kernel, axis, steps),
        grid_spec=pltpu.PrefetchScalarGridSpec(
            num_scalar_prefetch=1,
            grid=(len(blocks),),
            in_specs=[whole, whole, cotan, cotan]
            + [pl.BlockSpec(memory_space=pl.ANY)] * len(after),
            out_specs=[pl.BlockSpec((r, COLS), lambda i, w: (0, i)) for r in rows]
            + [pl.BlockSpec((8, DK), lambda i, w: (0, 0))],
            scratch_shapes=[
                pltpu.VMEM((256 * len(steps), 2 * TOK), BF16),
                pltpu.VMEM((2 * TOK, COLS), BF16),
            ],
        ),
        out_shape=[jax.ShapeDtypeStruct((r, width), F32) for r in rows]
        + [jax.ShapeDtypeStruct((8, DK), F32)],
        compiler_params=params(PRODUCT_LIMIT),
        cost_estimate=cost(1e6, 1e6),
        name="products_" + axis,
    )(where, keep, got, own, other, *after)


def relay_kernel(a, b, *rest):
    out, token = rest[-2:]
    out[...] = a[...] + b[...]
    token[...] = jnp.zeros_like(token)


def relay(term, arrived, after):
    rows, width = term.shape
    spec = pl.BlockSpec((rows, COLS), lambda i: (0, i))
    return pl.pallas_call(
        relay_kernel,
        grid=(width // COLS,),
        in_specs=[spec] * 2 + [pl.BlockSpec(memory_space=pl.ANY)] * len(after),
        out_specs=[spec, pl.BlockSpec((8, DK), lambda i: (0, 0))],
        out_shape=[
            jax.ShapeDtypeStruct(term.shape, F32),
            jax.ShapeDtypeStruct((8, DK), F32),
        ],
        input_output_aliases={0: 0},
        compiler_params=params(SMALL_LIMIT),
        cost_estimate=cost(rows * width, 12 * rows * width),
        name="relay",
    )(term, arrived, *after)


def second_kernel(axis, me, where_ref, mine, *rest):
    came, outs, total = rest[:-5], rest[-5:-1], rest[-1]
    core = where_ref[3]
    total[...] = sum((ref[...] for ref in came), mine[...])
    for t in range(4):
        step = (OPPOSITE, BEFORE, AFTER, MINE)[t]
        j = lax.rem(where_ref[me] + step(core), 4)
        if axis == "z":
            for y in range(4):
                row = pl.multiple_of(64 * y + 16 * j, 16)
                outs[t][16 * y : 16 * (y + 1), :] = total[pl.ds(row, 16), :]
        else:
            outs[t][...] = total[pl.ds(pl.multiple_of(64 * j, 64), 64), :]


def pass_kernel(where_ref, forth, came, *rest):
    rest[-2][...] = forth[...] + came[...]
    rest[-1][...] = sum((ref[...] for ref in rest[1:-2]), rest[0][...])


def halves_kernel(me, place, where_ref, a, *rest):
    came, (keep, away, total) = rest[:-3], rest[-3:]
    total[...] = sum((ref[...] for ref in came), a[...])
    rows = keep.shape[0]
    row = rows * place(where_ref[me])
    keep[...] = total[pl.ds(pl.multiple_of(row, rows), rows), :]
    away[...] = total[pl.ds(pl.multiple_of(rows - row, rows), rows), :]


def last_kernel(where_ref, *refs):
    out = refs[-1]
    col = 0
    for a, b in zip(refs[0:6:2], refs[1:6:2]):
        width = a.shape[1]
        out[:, col : col + width] = a[...] + b[...]
        col += width


def together(kernels, where, ins, outs, scratch, name):
    def body(where_ref, *refs):
        sets = [[] for _ in kernels]
        at = 0
        for lists in (ins, outs, scratch):
            for mine, part in zip(sets, lists):
                mine += refs[at : at + len(part)]
                at += len(part)
        for kernel, mine in zip(kernels, sets):
            kernel(where_ref, *mine)

    flat = lambda lists: [item for part in lists for item in part]
    results = iter(small_call(body, where, flat(ins), flat(outs), flat(scratch), (), name))
    return [[next(results) for _ in part] for part in outs]


def around(pieces, axis):
    return [pieces[0]] + [send(pieces[d], axis, d) for d in (1, 3, 2)]


def assemble_kernel(where_ref, *refs):
    for ref, d in zip(refs, (0, 1, 3, 2)):
        row = pl.multiple_of(lax.rem(where_ref[0] - d + 4, 4) * 16, 16)
        refs[-1][pl.ds(row, 16), :] = ref[...]


def shards(queries, key_rows, value_rows, log_gate, out_gate, cotangent):
    place = {name: lax.axis_index(name) for name in AXES}
    where = jnp.stack([place[name] for name in AXES]).astype(jnp.int32)
    q, k, v, g = queries[0], key_rows[0], value_rows[0], log_gate[0]
    own = cotangent[0]

    mine, got, local, other = attend(where, q, k, v, g, own)
    hidden, keep, away = gated(where, local, mine, got, out_gate[0])
    theirs = send(away, "c", 1).reshape(4, 4, 4, 16, TOK)
    keep = keep.reshape(4, 4, 4, 16, TOK)

    forward, backward = (lambda c: 1 - 2 * c), (lambda c: 2 * c - 1)
    order = ("x", "y", "z")
    terms, came = {}, {}
    token = ()
    for axis in ("y", "z", "x"):
        first = (BEFORE,) if axis == "x" else (OPPOSITE,)
        term, *token = products(axis, first, where, keep, theirs, own, other, token)
        came[axis] = send(term, axis, forward)
    for axis in ("x", "y", "z"):
        others = (OPPOSITE, AFTER, MINE) if axis == "x" else (BEFORE, AFTER, MINE)
        *terms[axis], t = products(axis, others, where, keep, theirs, own, other, token)
        token = [t]

    def pass_on(axis, n, after):
        term, *after = relay(terms[axis][n], came[axis], after)
        came[axis] = send(term, axis, forward)
        return after

    direct = {axis: (send(terms[axis][0], axis, backward),) for axis in ("y", "z")}
    direct["x"] = ()
    token = pass_on("x", 0, token)
    token = pass_on("y", 1, token)
    token = pass_on("z", 1, token)
    token = pass_on("x", 1, token)

    following = {"x": ("y", "z"), "y": ("z", "x"), "z": ("x", "y")}
    width = {axis: COLS * len(KINDS[axis]) for axis in order}
    parts = together(
        [functools.partial(second_kernel, a, AXES.index(following[a][0])) for a in order],
        where,
        [[terms[a][2], came[a], *direct[a]] for a in order],
        [[(64, width[a])] * 4 for a in order],
        [[(256, width[a])] for a in order],
        "second",
    )
    parts = dict(zip(order, parts))
    came = {a: send(parts[a][0], following[a][0], forward) for a in ("y", "z", "x")}
    straight = {a: [send(parts[a][1], following[a][0], backward)] for a in ("y", "z")}
    passed = together(
        [pass_kernel] * 3,
        where,
        [
            [parts[a][2], came[a]] + ([parts[a][3]] + straight[a] if a != "x" else [parts[a][1]])
            for a in order
        ],
        [[(64, width[a])] * 2 for a in order],
        [[]] * 3,
        "pass_on",
    )
    pairs = []
    for (forth, mine), a in zip(passed, order):
        arrived = [send(forth, following[a][0], forward)]
        if a == "x":
            mine, arrived = parts[a][3], arrived + [send(mine, following[a][0], backward)]
        pairs.append([mine] + arrived)
    upper, odd = (lambda p: lax.div(p, 2)), (lambda p: lax.rem(p, 2))
    for rows, distance, place_of in ((32, 2, upper), (16, 1, odd)):
        pairs = together(
            [
                functools.partial(halves_kernel, AXES.index(following[a][1]), place_of)
                for a in order
            ],
            where,
            pairs,
            [[(rows, width[a])] * 2 for a in order],
            [[(2 * rows, width[a])] for a in order],
            "halves",
        )
        pairs = [
            [keep, swap(away, following[a][1], distance)]
            for (keep, away), a in zip(pairs, order)
        ]
    rounds = dict(zip(order, pairs))
    (mine,) = small_call(
        last_kernel, where, [r for axis in KINDS for r in rounds[axis]], [(16, D)], name="last"
    )
    pieces = around([mine] * 4, "x")
    weight_grad = pl.pallas_call(
        assemble_kernel,
        in_specs=[pl.BlockSpec(memory_space=pltpu.SMEM)]
        + [pl.BlockSpec(memory_space=pltpu.VMEM)] * len(pieces),
        out_specs=pl.BlockSpec(memory_space=pltpu.VMEM),
        out_shape=jax.ShapeDtypeStruct((64, D), F32),
        compiler_params=pltpu.CompilerParams(vmem_limit_bytes=SMALL_LIMIT),
        cost_estimate=cost(64 * D, 8 * 64 * D),
        name="assemble",
    )(where, *pieces)
    return hidden[None], weight_grad


def solution(mesh):
    fine = Mesh(mesh.devices.reshape(SIZES), AXES)
    rows = P("x", ("y", "z", "c"), None)
    return jax.shard_map(
        shards,
        mesh=fine,
        in_specs=(rows,) * 6,
        out_specs=(rows, P(("y", "z", "c"), None)),
        check_vma=False,
    )
```

```python
import functools

import jax
import jax.numpy as jnp
from jax import lax
from jax.experimental import pallas as pl
from jax.experimental.pallas import tpu as pltpu
from jax.sharding import Mesh, PartitionSpec as P

H = 16
DK = 128
D = 4096
BLOCK = 64
TOK = 512
BLOCKS = TOK // BLOCK
HALF = DK // 2
MSG = HALF + 8
COLS = 512
AXES = ("x", "y", "z", "c")
SIZES = (4, 4, 4, 2)
F32 = jnp.float32
BF16 = jnp.bfloat16
VMEM_LIMIT = 60 * 1024 * 1024
PIECE_LIMIT = 24 * 1024 * 1024
PRODUCT_LIMIT = 28 * 1024 * 1024
SMALL_LIMIT = 16 * 1024 * 1024

KINDS = {"y": (0, 1, 2), "z": (3, 4, 5), "x": (6, 7)}
GROUP = 4


def linear(p):
    return ((p[0] * 4 + p[1]) * 4 + p[2]) * 2 + p[3]


def places():
    return [(x, y, z, c) for x in range(4) for y in range(4) for z in range(4) for c in range(2)]


def shift_pairs(axis, by):
    at = AXES.index(axis)
    pairs = []
    for p in places():
        q = list(p)
        step = by(p[3]) if callable(by) else by
        q[at] = (q[at] + step) % SIZES[at]
        pairs.append((linear(p), linear(q)))
    return pairs


def swap(array, axis, distance):
    at = AXES.index(axis)
    pairs = []
    for p in places():
        q = list(p)
        q[at] ^= distance
        pairs.append((linear(p), linear(q)))
    return lax.ppermute(array, AXES, pairs)


def send(array, axis, by):
    return lax.ppermute(array, AXES, shift_pairs(axis, by))


def params(limit=VMEM_LIMIT):
    return pltpu.CompilerParams(dimension_semantics=("arbitrary",), vmem_limit_bytes=limit)


def cost(flops, nbytes, transcendentals=0):
    return pl.CostEstimate(
        flops=int(flops), bytes_accessed=int(nbytes), transcendentals=int(transcendentals)
    )


def split(a):
    high = a.astype(BF16)
    return high, (a - high.astype(F32)).astype(BF16)


def dot_nt(a, b):
    return lax.dot_general(a, b, (((1,), (1,)), ((), ())), preferred_element_type=F32)


def dot_tn(a, b):
    return lax.dot_general(a, b, (((0,), (0,)), ((), ())), preferred_element_type=F32)


def dot_nt3(ah, al, b):
    n = ah.shape[0]
    high, low = split(b)
    both = dot_nt(jnp.concatenate([ah, al], axis=0), jnp.concatenate([high, low], axis=0))
    m = b.shape[0]
    return both[:n, :m] + (both[:n, m:] + both[n:, :m])


def block_cumsum(g):
    x = g.reshape(TOK // 8, 8, DK)
    row = lax.broadcasted_iota(jnp.int32, x.shape, 1)
    for shift in (1, 2, 4):
        x = x + jnp.where(row >= shift, pltpu.roll(x, shift, 1), 0.0)
    x = x.reshape(BLOCKS, BLOCK // 8, 8, DK)
    parts = []
    run = None
    for i in range(BLOCK // 8):
        part = x[:, i]
        if run is not None:
            part = part + run
        parts.append(part)
        run = part[:, 7:8, :]
    return jnp.stack(parts, axis=1).reshape(BLOCKS, BLOCK, DK), run


def state_kernel(
    where_ref, k_ref, v_ref, g_ref, cotan_ref, keep_ref, send_ref, cum_ref, wide_ref
):
    first = where_ref[3] == 0
    wide_ref[...] = cotan_ref[...].astype(F32)
    for head in range(GROUP):
        lanes = slice(head * DK, (head + 1) * DK)
        cum, end = block_cumsum(g_ref[:, lanes])
        cum_ref[:, lanes] = cum.reshape(TOK, DK)
        k = k_ref[:, lanes].astype(F32).reshape(BLOCKS, BLOCK, DK)
        kend = (k * jnp.exp(end - cum)).astype(BF16)
        decay = jnp.exp(end)
        total = end[0]
        state = None
        for j in range(BLOCKS):
            term = dot_tn(v_ref[j * BLOCK : (j + 1) * BLOCK, lanes], kend[j])
            if j:
                state = state * decay[j] + term
                total = total + end[j]
            else:
                state = term
        row = jnp.broadcast_to(jnp.exp(total), (8, DK))
        low, high = state[:HALF], state[HALF:]
        keep_ref[head, :HALF] = jnp.where(first, low, high)
        send_ref[head, :HALF] = jnp.where(first, high, low)
        keep_ref[head, HALF:] = row
        send_ref[head, HALF:] = row


def local_state(where, k, v, g, cotan):
    out = jax.ShapeDtypeStruct((H, MSG, DK), F32)
    steps = H // GROUP
    heads = pl.BlockSpec((TOK, GROUP * DK), lambda h, w: (0, h))
    wide = pl.BlockSpec((TOK, D // steps), lambda h, w: (0, h))
    return pl.pallas_call(
        state_kernel,
        grid_spec=pltpu.PrefetchScalarGridSpec(
            num_scalar_prefetch=1,
            grid=(steps,),
            in_specs=[heads] * 3 + [wide],
            out_specs=[pl.BlockSpec((GROUP, MSG, DK), lambda h, w: (h, 0, 0))] * 2
            + [heads, wide],
        ),
        out_shape=[out, out]
        + [jax.ShapeDtypeStruct((TOK, n), F32) for n in (H * DK, D)],
        compiler_params=params(PIECE_LIMIT),
        cost_estimate=cost(2 * TOK * DK * DK * H, 26e6, TOK * DK * H),
        name="local_state",
    )(where, k, v, g, cotan)


def core_kernel(q_ref, k_ref, v_ref, cum_ref, *rest):
    out_ref, high_ref, low_ref, token_ref = rest[-4:]
    token_ref[...] = jnp.zeros_like(token_ref)
    shape = (BLOCKS, BLOCK, DK)
    two = 2 * BLOCK
    rows = lax.broadcasted_iota(jnp.int32, (two, two), 0)
    cols = lax.broadcasted_iota(jnp.int32, (two, two), 1)
    mask = (rows >= cols) & ((rows >= BLOCK) == (cols >= BLOCK))
    for head in range(GROUP):
        lanes = slice(head * DK, (head + 1) * DK)
        cum = cum_ref[:, lanes].reshape(shape)
        end = cum[:, BLOCK - 1 : BLOCK, :]
        q = q_ref[:, lanes].astype(F32).reshape(shape)
        k = k_ref[:, lanes].astype(F32).reshape(shape)
        qdec = q * jnp.exp(cum)
        qround = qdec.astype(BF16)
        qrest = (qdec - qround.astype(F32)).astype(BF16)
        decay = jnp.exp(end)
        kfull = k * jnp.exp(-cum)
        kinc = kfull.astype(BF16)
        kend = (kfull * decay).astype(BF16)
        before = jnp.zeros((1, DK), F32)
        state = None
        for pair in range(BLOCKS // 2):
            span = slice(pair * two, (pair + 1) * two)
            qq = qround[2 * pair : 2 * pair + 2].reshape(two, DK)
            kk = kinc[2 * pair : 2 * pair + 2].reshape(two, DK)
            weights = jnp.where(mask, dot_nt(qq, kk), 0.0).astype(BF16)
            intra = jnp.dot(weights, v_ref[span, lanes], preferred_element_type=F32)
            for half in range(2):
                j = 2 * pair + half
                at = slice(j * BLOCK, (j + 1) * BLOCK)
                mine = intra[half * BLOCK : (half + 1) * BLOCK]
                if state is not None:
                    mine = mine + dot_nt3(qround[j], qrest[j], state)
                out_ref[at, lanes] = mine
                far = qdec[j] * jnp.exp(before)
                high, low = split(far)
                high_ref[at, lanes] = high
                low_ref[at, lanes] = low
                before = before + end[j]
                if j < BLOCKS - 1:
                    term = dot_tn(v_ref[at, lanes], kend[j])
                    state = term if state is None else state * decay[j] + term


def local_core(first, steps, q, k, v, cum, after, earlier):
    spec = pl.BlockSpec((TOK, GROUP * DK), lambda h: (0, h + first))
    extra = list(earlier) + [after]
    shape = (TOK, H * DK)
    return pl.pallas_call(
        core_kernel,
        grid=(steps,),
        in_specs=[spec] * 4 + [pl.BlockSpec(memory_space=pl.ANY)] * len(extra),
        out_specs=[spec] * 3 + [pl.BlockSpec((8, DK), lambda h: (0, 0))],
        out_shape=[jax.ShapeDtypeStruct(shape, t) for t in (F32, BF16, BF16)]
        + [jax.ShapeDtypeStruct((8, DK), F32)],
        input_output_aliases={4 + i: i for i in range(len(earlier))},
        compiler_params=params(PIECE_LIMIT),
        cost_estimate=cost(64 * TOK * DK * DK, 20e6, 16 * TOK * DK),
        name="local_core",
    )(q, k, v, cum, *extra)


def chip_kernel(where_ref, keep_ref, got_ref, wide_ref, *outs):
    z, c = where_ref[2], where_ref[3]
    first = c == 0
    for d in range(4):
        base = lax.rem(z + d, 4) * 4
        a = keep_ref[pl.ds(base, 4)]
        b = got_ref[pl.ds(base, 4)]
        early = jnp.where(first, a, b)
        late = jnp.where(first, b, a)
        decay = late[:, HALF : HALF + 1, :]
        outs[d][:, :HALF] = early[:, :HALF] * decay + late[:, :HALF]
        outs[d][:, HALF:] = early[:, HALF:] * late[:, HALF:]


def row_kernel(where_ref, r0, r1, r2, r3, prefix_ref, total_ref, hold):
    z = where_ref[2]
    for d, ref in zip((0, 1, 3, 2), (r0, r1, r2, r3)):
        hold[lax.rem(z - d + 4, 4)] = ref[...]
    state = jnp.zeros((4, HALF, DK), F32)
    decay = jnp.ones((4, 8, DK), F32)
    for i in range(4):
        prefix_ref[i, :, :HALF] = state
        prefix_ref[i, :, HALF:] = decay
        item = hold[i]
        late = item[:, HALF:]
        state = state * late[:, :1, :] + item[:, :HALF]
        decay = decay * late
    total_ref[:, :HALF] = state
    total_ref[:, HALF:] = decay


def back_kernel(where_ref, prefix_ref, r0, r1, r2, r3, *rest):
    outs, hold = rest[:4], rest[4]
    y, z = where_ref[1], where_ref[2]
    for d, ref in zip((0, 1, 3, 2), (r0, r1, r2, r3)):
        hold[lax.rem(y - d + 4, 4)] = ref[...]
    state = jnp.zeros((4, HALF, DK), F32)
    for i in range(3):
        item = hold[i]
        new = state * item[:, HALF : HALF + 1, :] + item[:, :HALF]
        state = jnp.where(i < y, new, state)
    for d in range(4):
        prefix = prefix_ref[lax.rem(z + d, 4)]
        outs[d][...] = state * prefix[:, HALF : HALF + 1, :] + prefix[:, :HALF]


def core_start_kernel(where_ref, keep_ref, got_ref, r0, r1, r2, r3, mine_ref, other_ref):
    z, c = where_ref[2], where_ref[3]
    first = c == 0
    for d, ref in zip((0, 1, 3, 2), (r0, r1, r2, r3)):
        at = pl.ds(lax.rem(z - d + 4, 4) * 4, 4)
        chip = ref[...]
        early = jnp.where(first, keep_ref[at], got_ref[at])
        second = chip * early[:, HALF : HALF + 1, :] + early[:, :HALF]
        mine_ref[at] = jnp.where(first, chip, second)
        other_ref[at] = jnp.where(first, second, chip)


def small_call(kernel, where, arrays, outs, scratch=(), after=(), name=None):
    whole = [pl.BlockSpec(memory_space=pltpu.VMEM)]
    nbytes = sum(a.size * 4 for a in arrays)
    used = 1 + len(arrays)

    def body(*refs):
        kernel(*refs[:used], *refs[used + len(after) :])

    return pl.pallas_call(
        body,
        in_specs=[pl.BlockSpec(memory_space=pltpu.SMEM)]
        + whole * len(arrays)
        + [pl.BlockSpec(memory_space=pl.ANY)] * len(after),
        out_specs=whole * len(outs),
        out_shape=[jax.ShapeDtypeStruct(s, F32) for s in outs],
        scratch_shapes=[pltpu.VMEM(s, F32) for s in scratch],
        compiler_params=pltpu.CompilerParams(vmem_limit_bytes=SMALL_LIMIT),
        cost_estimate=cost(nbytes, 2 * nbytes),
        name=name,
    )(where, *arrays, *after)


def chip_total(where, keep, got, wide):
    vmem = pl.BlockSpec(memory_space=pltpu.VMEM)
    away = pl.BlockSpec(memory_space=pl.ANY)
    return pl.pallas_call(
        chip_kernel,
        in_specs=[pl.BlockSpec(memory_space=pltpu.SMEM), vmem, vmem, away],
        out_specs=[vmem] * 4 + [away],
        out_shape=[jax.ShapeDtypeStruct((4, MSG, DK), F32)] * 4
        + [jax.ShapeDtypeStruct(wide.shape, F32)],
        input_output_aliases={3: 4},
        compiler_params=pltpu.CompilerParams(vmem_limit_bytes=SMALL_LIMIT),
        cost_estimate=cost(H * MSG * DK * 4, 16 * H * MSG * DK),
        name="chip_total",
    )(where, keep, got, wide)


def attend(where, q, k, v, g, own):
    keep, away, cum, wide = local_state(where, k, v, g, own)
    got = send(away, "c", 1)
    msg = (4, MSG, DK)
    *parts, wide = chip_total(where, keep, got, wide)
    other = send(wide, "c", 1)
    arrived = around(parts, "z")
    *local, token = local_core(0, 2, q, k, v, cum, parts[1], ())
    prefix, total = small_call(
        row_kernel, where, arrived, [(4,) + msg, msg], [(4,) + msg], [token], "row_total"
    )
    rows = around([total] * 4, "y")
    *local, token = local_core(2, 1, q, k, v, cum, total, local)
    out = (4, HALF, DK)
    back = small_call(
        back_kernel, where, [prefix] + rows, [out] * 4, [(4,) + msg], [token], "row_start"
    )
    arrived = around(back, "z")
    *local, token = local_core(3, 1, q, k, v, cum, back[1], local)
    mine, theirs = small_call(
        core_start_kernel,
        where,
        [keep, got] + arrived,
        [(H, HALF, DK)] * 2,
        after=[token],
        name="core_start",
    )
    return mine, send(theirs, "c", 1), local, other


def hidden_kernel(
    where_ref, out_ref, high_ref, low_ref, mine_ref, got_ref, gate_ref, hid_ref, keep_ref, send_ref
):
    first = where_ref[3] == 0
    for head in range(GROUP):
        lanes = slice(head * DK, (head + 1) * DK)
        a, b = mine_ref[head], got_ref[head]
        state = jnp.concatenate([jnp.where(first, a, b), jnp.where(first, b, a)], axis=0)
        core = out_ref[:, lanes] + dot_nt3(high_ref[:, lanes], low_ref[:, lanes], state)
        mean = jnp.mean(core * core, axis=-1, keepdims=True)
        gate = 0.5 * gate_ref[:, lanes].astype(F32)
        swish = gate + gate * jnp.tanh(gate)
        hidden = (core * lax.rsqrt(mean + 1e-05) * swish).astype(BF16)
        hid_ref[:, lanes] = hidden
        turned = hidden.astype(F32).T
        low, high = turned[:HALF], turned[HALF:]
        rows = slice(head * HALF, (head + 1) * HALF)
        keep_ref[rows, :] = jnp.where(first, low, high).astype(BF16)
        send_ref[rows, :] = jnp.where(first, high, low)


def gated(where, local, mine, got, gate):
    spec = pl.BlockSpec((TOK, GROUP * DK), lambda h, w: (0, h))
    state = pl.BlockSpec((GROUP, HALF, DK), lambda h, w: (h, 0, 0))
    turned = pl.BlockSpec((GROUP * HALF, TOK), lambda h, w: (h, 0))
    return pl.pallas_call(
        hidden_kernel,
        grid_spec=pltpu.PrefetchScalarGridSpec(
            num_scalar_prefetch=1,
            grid=(H // GROUP,),
            in_specs=[spec, spec, spec, state, state, spec],
            out_specs=[spec, turned, turned],
        ),
        out_shape=[
            jax.ShapeDtypeStruct((TOK, H * DK), BF16),
            jax.ShapeDtypeStruct((H * HALF, TOK), BF16),
            jax.ShapeDtypeStruct((H * HALF, TOK), F32),
        ],
        compiler_params=params(PIECE_LIMIT),
        cost_estimate=cost(6 * TOK * DK * DK * H, 17e6, 2 * TOK * DK * H),
        name="gated_hidden",
    )(where, *local, mine, got, gate)


CHUNK = {"x": (4, 4, 1, 16, TOK), "y": (1, 4, 4, 16, TOK), "z": (4, 1, 4, 16, TOK)}


def product_kernel(axis, steps, where_ref, keep_ref, got_ref, own_ref, other_ref, *refs):
    *outs, token_ref, left_ref, right_ref = refs[-3 - len(steps) :]
    core = where_ref[3]
    token_ref[...] = jnp.zeros_like(token_ref)

    def chunk(ref, j):
        if axis == "y":
            return ref[j]
        if axis == "z":
            return ref[:, j]
        return ref[:, :, j]

    @pl.when(pl.program_id(0) == 0)
    def _():
        me = where_ref[AXES.index(axis)]
        for t, step in enumerate(steps):
            j = lax.rem(me + step(core), 4)
            for part, ref in enumerate((keep_ref, got_ref)):
                lanes = slice(part * TOK, (part + 1) * TOK)
                rows = chunk(ref, j).reshape(256, TOK)
                left_ref[256 * t : 256 * (t + 1), lanes] = rows.astype(BF16)

    right_ref[:TOK, :] = own_ref[...]
    right_ref[TOK:, :] = other_ref[...].astype(BF16)
    total = jnp.dot(left_ref[...], right_ref[...], preferred_element_type=F32)
    for t, out in enumerate(outs):
        out[...] = total[256 * t : 256 * (t + 1)]


BEFORE, OPPOSITE = (lambda core: 3 - 2 * core), (lambda core: 2)
AFTER, MINE = (lambda core: 1 + 2 * core), (lambda core: 0)


def products(axis, steps, where, keep, got, own, other, after):
    blocks = KINDS[axis]
    rows = (256,) * len(steps)
    cotan = pl.BlockSpec((TOK, COLS), lambda i, w: (0, blocks[0] + i))
    whole = pl.BlockSpec((4, 4, 4, 16, TOK), lambda i, w: (0, 0, 0, 0, 0))
    width = COLS * len(blocks)
    return pl.pallas_call(
        functools.partial(product_kernel, axis, steps),
        grid_spec=pltpu.PrefetchScalarGridSpec(
            num_scalar_prefetch=1,
            grid=(len(blocks),),
            in_specs=[whole, whole, cotan, cotan]
            + [pl.BlockSpec(memory_space=pl.ANY)] * len(after),
            out_specs=[pl.BlockSpec((r, COLS), lambda i, w: (0, i)) for r in rows]
            + [pl.BlockSpec((8, DK), lambda i, w: (0, 0))],
            scratch_shapes=[
                pltpu.VMEM((256 * len(steps), 2 * TOK), BF16),
                pltpu.VMEM((2 * TOK, COLS), BF16),
            ],
        ),
        out_shape=[jax.ShapeDtypeStruct((r, width), F32) for r in rows]
        + [jax.ShapeDtypeStruct((8, DK), F32)],
        compiler_params=params(PRODUCT_LIMIT),
        cost_estimate=cost(1e6, 1e6),
        name="products_" + axis,
    )(where, keep, got, own, other, *after)


def relay_kernel(a, b, *rest):
    out, token = rest[-2:]
    out[...] = a[...] + b[...]
    token[...] = jnp.zeros_like(token)


def relay(term, arrived, after):
    rows, width = term.shape
    spec = pl.BlockSpec((rows, COLS), lambda i: (0, i))
    return pl.pallas_call(
        relay_kernel,
        grid=(width // COLS,),
        in_specs=[spec] * 2 + [pl.BlockSpec(memory_space=pl.ANY)] * len(after),
        out_specs=[spec, pl.BlockSpec((8, DK), lambda i: (0, 0))],
        out_shape=[
            jax.ShapeDtypeStruct(term.shape, F32),
            jax.ShapeDtypeStruct((8, DK), F32),
        ],
        input_output_aliases={0: 0},
        compiler_params=params(SMALL_LIMIT),
        cost_estimate=cost(rows * width, 12 * rows * width),
        name="relay",
    )(term, arrived, *after)


def second_kernel(axis, me, where_ref, mine, *rest):
    came, outs, total = rest[:-5], rest[-5:-1], rest[-1]
    core = where_ref[3]
    total[...] = sum((ref[...] for ref in came), mine[...])
    for t in range(4):
        step = (OPPOSITE, BEFORE, AFTER, MINE)[t]
        j = lax.rem(where_ref[me] + step(core), 4)
        if axis == "z":
            for y in range(4):
                row = pl.multiple_of(64 * y + 16 * j, 16)
                outs[t][16 * y : 16 * (y + 1), :] = total[pl.ds(row, 16), :]
        else:
            outs[t][...] = total[pl.ds(pl.multiple_of(64 * j, 64), 64), :]


def pass_kernel(where_ref, forth, came, *rest):
    rest[-2][...] = forth[...] + came[...]
    rest[-1][...] = sum((ref[...] for ref in rest[1:-2]), rest[0][...])


def halves_kernel(me, place, where_ref, a, *rest):
    came, (keep, away, total) = rest[:-3], rest[-3:]
    total[...] = sum((ref[...] for ref in came), a[...])
    rows = keep.shape[0]
    row = rows * place(where_ref[me])
    keep[...] = total[pl.ds(pl.multiple_of(row, rows), rows), :]
    away[...] = total[pl.ds(pl.multiple_of(rows - row, rows), rows), :]


def last_kernel(where_ref, *refs):
    out = refs[-1]
    col = 0
    for a, b in zip(refs[0:6:2], refs[1:6:2]):
        width = a.shape[1]
        out[:, col : col + width] = a[...] + b[...]
        col += width


def together(kernels, where, ins, outs, scratch, name):
    def body(where_ref, *refs):
        sets = [[] for _ in kernels]
        at = 0
        for lists in (ins, outs, scratch):
            for mine, part in zip(sets, lists):
                mine += refs[at : at + len(part)]
                at += len(part)
        for kernel, mine in zip(kernels, sets):
            kernel(where_ref, *mine)

    flat = lambda lists: [item for part in lists for item in part]
    results = iter(small_call(body, where, flat(ins), flat(outs), flat(scratch), (), name))
    return [[next(results) for _ in part] for part in outs]


def around(pieces, axis):
    return [pieces[0]] + [send(pieces[d], axis, d) for d in (1, 3, 2)]


def assemble_kernel(where_ref, *refs):
    for ref, d in zip(refs, (0, 1, 3, 2)):
        row = pl.multiple_of(lax.rem(where_ref[0] - d + 4, 4) * 16, 16)
        refs[-1][pl.ds(row, 16), :] = ref[...]


def shards(queries, key_rows, value_rows, log_gate, out_gate, cotangent):
    place = {name: lax.axis_index(name) for name in AXES}
    where = jnp.stack([place[name] for name in AXES]).astype(jnp.int32)
    q, k, v, g = queries[0], key_rows[0], value_rows[0], log_gate[0]
    own = cotangent[0]

    mine, got, local, other = attend(where, q, k, v, g, own)
    hidden, keep, away = gated(where, local, mine, got, out_gate[0])
    theirs = send(away, "c", 1).reshape(4, 4, 4, 16, TOK)
    keep = keep.reshape(4, 4, 4, 16, TOK)

    forward, backward = (lambda c: 1 - 2 * c), (lambda c: 2 * c - 1)
    order = ("x", "y", "z")
    terms, came = {}, {}
    token = ()
    for axis in ("y", "z", "x"):
        first = (BEFORE,) if axis == "x" else (OPPOSITE,)
        term, *token = products(axis, first, where, keep, theirs, own, other, token)
        came[axis] = send(term, axis, forward)
    for axis in ("x", "y", "z"):
        others = (OPPOSITE, AFTER, MINE) if axis == "x" else (BEFORE, AFTER, MINE)
        *terms[axis], t = products(axis, others, where, keep, theirs, own, other, token)
        token = [t]

    def pass_on(axis, n, after):
        term, *after = relay(terms[axis][n], came[axis], after)
        came[axis] = send(term, axis, forward)
        return after

    direct = {axis: (send(terms[axis][0], axis, backward),) for axis in ("y", "z")}
    direct["x"] = ()
    token = pass_on("x", 0, token)
    token = pass_on("y", 1, token)
    token = pass_on("z", 1, token)
    token = pass_on("x", 1, token)

    following = {"x": ("y", "z"), "y": ("z", "x"), "z": ("x", "y")}
    width = {axis: COLS * len(KINDS[axis]) for axis in order}
    parts = together(
        [functools.partial(second_kernel, a, AXES.index(following[a][0])) for a in order],
        where,
        [[terms[a][2], came[a], *direct[a]] for a in order],
        [[(64, width[a])] * 4 for a in order],
        [[(256, width[a])] for a in order],
        "second",
    )
    parts = dict(zip(order, parts))
    came = {a: send(parts[a][0], following[a][0], forward) for a in ("y", "z", "x")}
    straight = {a: [send(parts[a][1], following[a][0], backward)] for a in ("y", "z")}
    passed = together(
        [pass_kernel] * 3,
        where,
        [
            [parts[a][2], came[a]] + ([parts[a][3]] + straight[a] if a != "x" else [parts[a][1]])
            for a in order
        ],
        [[(64, width[a])] * 2 for a in order],
        [[]] * 3,
        "pass_on",
    )
    pairs = []
    for (forth, mine), a in zip(passed, order):
        arrived = [send(forth, following[a][0], forward)]
        if a == "x":
            mine, arrived = parts[a][3], arrived + [send(mine, following[a][0], backward)]
        pairs.append([mine] + arrived)
    upper, odd = (lambda p: lax.div(p, 2)), (lambda p: lax.rem(p, 2))
    for rows, distance, place_of in ((32, 2, upper), (16, 1, odd)):
        pairs = together(
            [
                functools.partial(halves_kernel, AXES.index(following[a][1]), place_of)
                for a in order
            ],
            where,
            pairs,
            [[(rows, width[a])] * 2 for a in order],
            [[(2 * rows, width[a])] for a in order],
            "halves",
        )
        pairs = [
            [keep, swap(away, following[a][1], distance)]
            for (keep, away), a in zip(pairs, order)
        ]
    rounds = dict(zip(order, pairs))
    (mine,) = small_call(
        last_kernel, where, [r for axis in KINDS for r in rounds[axis]], [(16, D)], name="last"
    )
    pieces = around([mine] * 4, "x")
    weight_grad = pl.pallas_call(
        assemble_kernel,
        in_specs=[pl.BlockSpec(memory_space=pltpu.SMEM)]
        + [pl.BlockSpec(memory_space=pltpu.VMEM)] * len(pieces),
        out_specs=pl.BlockSpec(memory_space=pltpu.VMEM),
        out_shape=jax.ShapeDtypeStruct((64, D), F32),
        compiler_params=pltpu.CompilerParams(vmem_limit_bytes=SMALL_LIMIT),
        cost_estimate=cost(64 * D, 8 * 64 * D),
        name="assemble",
    )(where, *pieces)
    return hidden[None], weight_grad


def solution(mesh):
    fine = Mesh(mesh.devices.reshape(SIZES), AXES)
    rows = P("x", ("y", "z", "c"), None)
    return jax.shard_map(
        shards,
        mesh=fine,
        in_specs=(rows,) * 6,
        out_specs=(rows, P(("y", "z", "c"), None)),
        check_vma=False,
    )
```
